128 devices in a mesh: chain: 8 (over x, core), sector: 16 (over z, y).
Axes of the slice: x: 4, y: 4, z: 4, core: 2. Of those that a mesh axis runs over, the one named last changes fastest.
Arguments:
- left_env: float32 [8, 16, 128, 128, 128], P('chain', None, 'sector'), may hold values from -3 to 3
- right_env: float32 [8, 16, 128, 128, 128], P('chain', None, 'sector'), may hold values from -3 to 3
- site_block: float32 [8, 128, 128, 128], P('chain', 'sector'), may hold values from -0.5 to 0.5
- start_vec: float32 [8, 128, 128, 128], P('chain', 'sector'), may hold values from -6 to 6
- slot_sector: int32 [128], replicated, may hold values from 0 to 127, each once
- couple: int32 [128, 16], replicated, may hold values from 0 to 127, as said below
- dims: int32 [128], replicated, may hold values from 64 to 128, as said below
- kept: int32 [128], replicated, may hold values from 0 to 1, as said below
Outputs:
- wave: float32 [8, 128, 128, 128], P('chain', 'sector')
- env_next: float32 [8, 16, 128, 128, 128], P('chain', None, 'sector')
- energy: float32 [8], P('chain')
The draws below stay inside these ranges and needn't reach their ends.
Inputs may be any that keep to these rules, and one draw needn't show every extreme that they name: `slot_sector`: a permutation of the sector ids. couple[s, 0] = s for every sector s (the on-site term). `dims`: at least one sector uses the full block. At least one sector is kept.
All inputs are finite; a program needn't handle non-finite values.
Results may differ from the reference program's by a relative error of at most 0.00013.
Values sent between devices are 32-bit elements; how exact they have to be, the bound alone decides.
No kernel may reach another device: no remote copies, remote signals or barrier semaphores. Data moves between devices by JAX's collectives and lax.ppermute only.
A program may use at most 128 MiB of HBM per device.

```python
import jax
import jax.numpy as jnp
from jax import lax

BLK = 128
W = 16
ITERS = 2
NSEC = 128
SEGS = 8


def draw_dims(key, part):
    key = jax.random.fold_in(key, 11)
    first, second = jax.random.split(key)
    values = jax.random.randint(first, (NSEC,), BLK // 2, BLK + 1).astype(jnp.int32)
    where = jax.random.randint(second, (), 0, NSEC)
    return values.at[where].set(BLK)


def draw_kept(key, part):
    key = jax.random.fold_in(key, 12)
    first, second = jax.random.split(key)
    values = (jax.random.randint(first, (NSEC,), 0, 4) > 0).astype(jnp.int32)
    where = jax.random.randint(second, (), 0, NSEC)
    return values.at[where].set(1)


def draw_couple(key, part):
    key = jax.random.fold_in(key, 13)
    values = jax.random.randint(key, (NSEC, W), 0, NSEC).astype(jnp.int32)
    onsite = jnp.arange(NSEC, dtype=jnp.int32)
    return values.at[:, 0].set(onsite)


def add_diagonal(noise_part, strength):
    row_place = jnp.arange(BLK)[:, None]
    column_place = jnp.arange(BLK)[None, :]
    identity = (row_place == column_place).astype(jnp.float32)
    leading = (jnp.arange(W) == 0).astype(jnp.float32)
    return noise_part + strength * leading[None, :, None, None, None] * identity[None, None, None, :, :]


def draw_left_env(key, part):
    key = jax.random.fold_in(key, 21)
    full_shape = (SEGS, W, NSEC, BLK, BLK)
    spread_scale = BLK ** (-0.5)
    noise_part = jnp.clip(jax.random.normal(key, full_shape, jnp.float32), -6.0, 6.0) * spread_scale
    strength = 0.6
    return add_diagonal(noise_part, strength)


def draw_right_env(key, part):
    key = jax.random.fold_in(key, 22)
    full_shape = (SEGS, W, NSEC, BLK, BLK)
    spread_scale = BLK ** (-0.5)
    noise_part = jnp.clip(jax.random.normal(key, full_shape, jnp.float32), -6.0, 6.0) * spread_scale
    strength = 0.6
    return add_diagonal(noise_part, strength)


def levels(key, shape, pieces, smallest, high):
    gain = 1.0
    for dim, blocks in pieces:
        steps = jax.random.uniform(jax.random.fold_in(jax.random.fold_in(key, 6), dim), (blocks,), jnp.float32, smallest / len(pieces), high / len(pieces))
        gain = gain * jnp.repeat(jnp.exp(steps), shape[dim] // blocks).reshape((-1,) + (1,) * (len(shape) - 1 - dim))
    return gain


def bell_draw(rng, shape, width, reach, cuts=(), kind=jnp.bfloat16):
    gain = levels(rng, shape, cuts, -0.22, 0.18) if cuts else 1.0
    drawn = jax.random.normal(rng, shape, jnp.float32) * width * gain
    return jnp.minimum(jnp.maximum(drawn, -reach), reach).astype(kind)


def setup_inputs(seed: int = 0) -> dict:
    key_list = jax.random.split(jax.random.key(seed), 9)
    left_env = draw_left_env(jax.random.fold_in(key_list[8], 71), 0)
    right_env = draw_right_env(jax.random.fold_in(key_list[8], 71), 0)
    site_block = bell_draw(key_list[2], (SEGS, NSEC, BLK, BLK), BLK ** -0.5, 0.5, ((0, 8), (1, 16)), jnp.float32)
    start_vec = bell_draw(key_list[3], (SEGS, NSEC, BLK, BLK), 1.0, 6.0, ((0, 8), (1, 16)), jnp.float32)
    slot_sector = jax.random.permutation(key_list[4], NSEC).astype(jnp.int32)
    couple = draw_couple(jax.random.fold_in(key_list[8], 71), 0)
    dims = draw_dims(jax.random.fold_in(key_list[8], 71), 0)
    kept = draw_kept(jax.random.fold_in(key_list[8], 71), 0)
    return dict(left_env=left_env, right_env=right_env, site_block=site_block, start_vec=start_vec, slot_sector=slot_sector, couple=couple, dims=dims, kept=kept)


HI = lax.Precision.HIGHEST

def update(lenv, site):
    half = jnp.einsum('wsab,sbj->wsaj', lenv, site, precision=HI)
    return jnp.einsum('sai,wsaj->wsij', site, half, precision=HI)

def reference(left_env, right_env, site_block, start_vec, slot_sector, couple, dims, kept):
    nsec = slot_sector.shape[0]
    inverse = jnp.zeros((nsec,), jnp.int32).at[slot_sector].set(jnp.arange(nsec, dtype=jnp.int32))
    source = inverse[couple[slot_sector]]
    limit = dims[slot_sector]
    inside = jnp.arange(BLK, dtype=jnp.int32)[None, :] < limit[:, None]
    mask = (inside[:, :, None] & inside[:, None, :]).astype(jnp.float32)
    mask = mask * kept[slot_sector].astype(jnp.float32)[:, None, None]
    env_next = lax.map(lambda pair: update(pair[0], pair[1]), (left_env, site_block))
    used = jnp.concatenate([left_env[:1], env_next[:-1]], axis=0)

    def solve(items):
        luse, renv, start = items

        def apply(vec):
            picked = vec[source]
            inner = jnp.einsum('swab,wsbc->swac', picked, renv, precision=HI)
            return mask * jnp.einsum('wsia,swac->sic', luse, inner, precision=HI)
        x = mask * start
        x = x / jnp.sqrt(jnp.sum(x * x) + 1e-06)
        y = apply(x)
        lam = jnp.float32(0.0)
        for step in range(ITERS):
            a = jnp.sum(x * y)
            resid = y - a * x
            b2 = jnp.sum(resid * resid) + 1e-06
            b = jnp.sqrt(b2)
            z = apply(resid)
            d = jnp.sum(resid * z) / b2
            lam = (a + d) / 2 - jnp.sqrt(((a - d) / 2) ** 2 + b2)
            q = lam - a
            n = jnp.sqrt(b2 + q * q)
            x = (b * x + q / b * resid) / n
            y = (b * y + q / b * z) / n
        return (x, lam)
    wave, energy = lax.map(solve, (used, right_env, start_vec))
    return (wave, env_next, energy)
```

```python
import functools

import jax
import jax.numpy as jnp
from jax import lax
from jax.experimental import pallas as pl
from jax.experimental.pallas import tpu as pltpu
from jax.sharding import PartitionSpec as P

MIB = 1 << 20


def split(value):
    high = value.astype(jnp.bfloat16)
    low = (value - high.astype(jnp.float32)).astype(jnp.bfloat16)
    return high, low


def dot(left, right):
    return jnp.dot(left, right, preferred_element_type=jnp.float32)


def right_factor(high, low):
    top = jnp.concatenate([high, low], axis=1)
    bottom = jnp.concatenate([high, jnp.zeros_like(low)], axis=1)
    return jnp.concatenate([top, bottom], axis=0)


def folded(value):
    half = value.shape[1] // 2
    return value[:, :half] + value[:, half:]


def update_kernel(left_ref, site_ref, out_ref):
    terms, _, blk, _ = left_ref.shape
    site = site_ref[0]
    factor = right_factor(*split(site))
    high, low = split(site.T)
    outer = jnp.concatenate([high, low, high], axis=1)
    for term in range(0, terms, 2):
        tops = []
        for index in (term, term + 1):
            first = jnp.concatenate(split(left_ref[index, 0]), axis=1)
            half_high, half_low = split(folded(dot(first, factor)))
            tops.append(jnp.concatenate([half_high, half_high, half_low], axis=0))
        both = dot(outer, jnp.concatenate(tops, axis=1))
        out_ref[term, 0] = both[:, :blk]
        out_ref[term + 1, 0] = both[:, blk:]


def update(left, site):
    terms, slots, blk, _ = left.shape
    return pl.pallas_call(
        update_kernel,
        out_shape=jax.ShapeDtypeStruct(left.shape, jnp.float32),
        grid=(slots,),
        in_specs=[
            pl.BlockSpec((terms, 1, blk, blk), lambda s: (0, s, 0, 0)),
            pl.BlockSpec((1, blk, blk), lambda s: (s, 0, 0)),
        ],
        out_specs=pl.BlockSpec((terms, 1, blk, blk), lambda s: (0, s, 0, 0)),
        compiler_params=pltpu.CompilerParams(vmem_limit_bytes=24 * MIB),
        cost_estimate=pl.CostEstimate(
            flops=8 * terms * slots * blk**3, bytes_accessed=8 * left.size, transcendentals=0
        ),
    )(left, site)


def apply_kernel(row_ref, vec_ref, left_ref, right_ref, mask_ref, out_ref, blocks, inner, sems):
    terms, _, blk, _ = left_ref.shape
    slot = pl.program_id(0)
    slots = pl.num_programs(0)

    def fetch(which, buffer, act):
        for term in range(terms):
            row = pl.multiple_of(row_ref[which, term], 8)
            copy = pltpu.make_async_copy(
                vec_ref.at[pl.ds(row, blk), :], blocks.at[buffer, term], sems.at[buffer]
            )
            if act == "start":
                copy.start()
            else:
                copy.wait()

    @pl.when(slot == 0)
    def _():
        fetch(0, 0, "start")

    @pl.when(slot + 1 < slots)
    def _():
        fetch(slot + 1, (slot + 1) % 2, "start")

    now = slot % 2
    fetch(slot, now, "wait")
    for term in range(terms):
        first = jnp.concatenate(split(blocks[now, term]), axis=1)
        value = folded(dot(first, right_factor(*split(right_ref[term, 0]))))
        rows = slice(term * blk, (term + 1) * blk)
        inner[rows, :] = jnp.concatenate(split(value), axis=1)
    total = jnp.zeros((2 * blk, 2 * blk), jnp.float32)
    for term in range(0, terms, 2):
        pairs = [split(left_ref[index, 0]) for index in (term, term + 1)]
        outer = jnp.concatenate(
            [
                jnp.concatenate([pairs[0][0], pairs[1][0]], axis=1),
                jnp.concatenate([pairs[0][1], pairs[1][1]], axis=1),
            ],
            axis=0,
        )
        total = total + dot(outer, inner[term * blk : (term + 2) * blk, :])
    result = total[:blk, :blk] + (total[blk:, :blk] + total[:blk, blk:])
    out_ref[0] = result * mask_ref[0]


def apply(rows, gathered, left, right, mask):
    terms, slots, blk, _ = left.shape
    return pl.pallas_call(
        apply_kernel,
        out_shape=jax.ShapeDtypeStruct((slots, blk, blk), jnp.float32),
        grid_spec=pltpu.PrefetchScalarGridSpec(
            num_scalar_prefetch=1,
            grid=(slots,),
            in_specs=[
                pl.BlockSpec(memory_space=pl.ANY),
                pl.BlockSpec((terms, 1, blk, blk), lambda s, r: (0, s, 0, 0)),
                pl.BlockSpec((terms, 1, blk, blk), lambda s, r: (0, s, 0, 0)),
                pl.BlockSpec((1, blk, blk), lambda s, r: (s, 0, 0)),
            ],
            out_specs=pl.BlockSpec((1, blk, blk), lambda s, r: (s, 0, 0)),
            scratch_shapes=[
                pltpu.VMEM((2, terms, blk, blk), jnp.float32),
                pltpu.VMEM((terms * blk, 2 * blk), jnp.bfloat16),
                pltpu.SemaphoreType.DMA((2,)),
            ],
        ),
        compiler_params=pltpu.CompilerParams(vmem_limit_bytes=24 * MIB),
        cost_estimate=pl.CostEstimate(
            flops=8 * terms * slots * blk**3, bytes_accessed=12 * left.size, transcendentals=0
        ),
    )(rows, gathered, left, right, mask)


def passed_along(value, axis, steps):
    count = lax.axis_size(axis)
    leading, last = (max(0, -steps), min(count, count - steps))
    return lax.ppermute(value, axis, [(source, source + steps) for source in range(leading, last)])


def body(left_env, right_env, site_block, start_vec, slot_sector, couple, dims, kept):
    lenv = left_env[0]
    renv = right_env[0]
    site = site_block[0]
    start = start_vec[0]
    sdev = start.shape[0]
    blk = start.shape[1]
    nsec = slot_sector.shape[0]
    owner = lax.axis_index("sector")
    slots = owner * sdev + jnp.arange(sdev, dtype=jnp.int32)
    sector_ids = jnp.take(slot_sector, slots)
    inverse = jnp.zeros((nsec,), jnp.int32).at[slot_sector].set(jnp.arange(nsec, dtype=jnp.int32))
    source = inverse[couple[sector_ids]]
    limit = dims[sector_ids]
    inside = jnp.arange(blk, dtype=jnp.int32)[None, :] < limit[:, None]
    mask = (inside[:, :, None] & inside[:, None, :]).astype(jnp.float32)
    mask = mask * kept[sector_ids].astype(jnp.float32)[:, None, None]
    updated = update(lenv, site)
    arrived = passed_along(updated, "chain", 1)
    luse = jnp.where(lax.axis_index("chain") == 0, lenv, arrived)
    height = sdev * blk + 8
    rows = (source // sdev) * height + (source % sdev) * blk

    def gather(vec, partial):
        tail = jnp.zeros((8, blk), jnp.float32)
        tail = tail.at[0, : len(partial)].set(jnp.stack(partial))
        packed = jnp.concatenate([vec.reshape(sdev * blk, blk), tail], axis=0)
        whole = lax.all_gather(packed, "sector", axis=0, tiled=True)
        sums = jnp.sum(whole.reshape(-1, height, blk)[:, sdev * blk, : len(partial)], axis=0)
        return whole, [sums[k] for k in range(len(partial))]

    def inner(one, other):
        return jnp.sum(one * other)

    begin = mask * start
    whole, (norm,) = gather(begin, [inner(begin, begin)])
    scale = 1.0 / jnp.sqrt(norm + 1e-06)
    x0 = begin * scale
    y0 = apply(rows, whole, luse, renv, mask) * scale
    whole, (a0,) = gather(y0, [inner(x0, y0)])
    w1 = apply(rows, whole, luse, renv, mask)
    r1 = y0 - a0 * x0
    z1 = w1 - a0 * y0
    whole, (xy, xz, ry, rz, rr) = gather(
        z1, [inner(x0, y0), inner(x0, z1), inner(r1, y0), inner(r1, z1), inner(r1, r1)]
    )

    def mix(a, b2, rz):
        b = jnp.sqrt(b2)
        d = rz / b2
        lam = (a + d) / 2 - jnp.sqrt(((a - d) / 2) ** 2 + b2)
        q = lam - a
        n = jnp.sqrt(b2 + q * q)
        return lam, b / n, (q / b) / n

    _, keep, turn = mix(a0, rr + 1e-06, rz)
    x1 = keep * x0 + turn * r1
    y1 = keep * y0 + turn * z1
    a1 = keep * keep * xy + keep * turn * (xz + ry) + turn * turn * rz
    r2 = y1 - a1 * x1
    w2 = apply(rows, whole, luse, renv, mask)
    z2 = keep * w1 + turn * w2 - a1 * y1
    rr, rz = lax.psum((inner(r2, r2), inner(r2, z2)), "sector")
    lam, keep, turn = mix(a1, rr + 1e-06, rz)
    x2 = keep * x1 + turn * r2
    return (x2[None], updated[None], jnp.reshape(lam, (1,)))


def solution(mesh):
    placed = (
        P("chain", None, "sector", None, None),
        P("chain", None, "sector", None, None),
        P("chain", "sector", None, None),
        P("chain", "sector", None, None),
        P(),
        P(),
        P(),
        P(),
    )
    return jax.shard_map(
        body,
        mesh=mesh,
        in_specs=placed,
        out_specs=(
            P("chain", "sector", None, None),
            P("chain", None, "sector", None, None),
            P("chain"),
        ),
        check_vma=False,
    )
```

```python
import functools

import jax
import jax.numpy as jnp
from jax import lax
from jax.experimental import pallas as pl
from jax.experimental.pallas import tpu as pltpu
from jax.sharding import PartitionSpec as P

MIB = 1 << 20
TAIL = 8
PARTS = 4
SIDE = 4
ORDERS = ((("y", 1), ("y", 3), ("z", 1), ("z", 3)), (("y", 3), ("y", 1), ("z", 3), ("z", 1)),
          (("z", 1), ("z", 3), ("y", 1), ("y", 3)), (("z", 3), ("z", 1), ("y", 3), ("y", 1)))


def split(value):
    high = value.astype(jnp.bfloat16)
    low = (value - high.astype(jnp.float32)).astype(jnp.bfloat16)
    return high, low


def dot(left, right):
    return jnp.dot(left, right, preferred_element_type=jnp.float32)


def right_factor(high, low):
    top = jnp.concatenate([high, low], axis=1)
    bottom = jnp.concatenate([high, jnp.zeros_like(low)], axis=1)
    return jnp.concatenate([top, bottom], axis=0)


def folded(value):
    half = value.shape[1] // 2
    return value[:, :half] + value[:, half:]


def update_kernel(left_ref, site_ref, out_ref):
    terms, _, blk, _ = left_ref.shape
    site = site_ref[0]
    factor = right_factor(*split(site))
    high, low = split(site.T)
    outer = jnp.concatenate([high, low, high], axis=1)
    for term in range(0, terms, 2):
        tops = []
        for index in (term, term + 1):
            first = jnp.concatenate(split(left_ref[index, 0]), axis=1)
            half_high, half_low = split(folded(dot(first, factor)))
            tops.append(jnp.concatenate([half_high, half_high, half_low], axis=0))
        both = dot(outer, jnp.concatenate(tops, axis=1))
        out_ref[term, 0] = both[:, :blk]
        out_ref[term + 1, 0] = both[:, blk:]


def update(left, site):
    terms, slots, blk, _ = left.shape
    return pl.pallas_call(
        update_kernel,
        out_shape=jax.ShapeDtypeStruct(left.shape, jnp.float32),
        grid=(slots,),
        in_specs=[
            pl.BlockSpec((terms, 1, blk, blk), lambda s: (0, s, 0, 0)),
            pl.BlockSpec((1, blk, blk), lambda s: (s, 0, 0)),
        ],
        out_specs=pl.BlockSpec((terms, 1, blk, blk), lambda s: (0, s, 0, 0)),
        compiler_params=pltpu.CompilerParams(vmem_limit_bytes=16 * MIB),
        cost_estimate=pl.CostEstimate(
            flops=8 * terms * slots * blk**3, bytes_accessed=8 * left.size, transcendentals=0
        ),
    )(left, site)


def masked(value, limit):
    rows = lax.broadcasted_iota(jnp.int32, value.shape, 0)
    columns = lax.broadcasted_iota(jnp.int32, value.shape, 1)
    return jnp.where(jnp.maximum(rows, columns) < limit, value, 0.0)


def put_quarter(slot, value, quarters):
    blk = value.shape[0]
    per = pl.num_programs(0) // PARTS
    at = pl.ds(pl.multiple_of((slot % per) * blk, blk), blk)
    for part, quarter in enumerate(quarters):
        @pl.when(slot // per == part)
        def _(quarter=quarter):
            quarter[at, :] = value


def put_sums(slot, products, tail):
    rows = [jnp.sum(product, axis=0, keepdims=True) for product in products]
    rows.append(jnp.zeros((TAIL - len(rows), rows[0].shape[1]), jnp.float32))
    block = jnp.concatenate(rows, axis=0)
    tail[...] = jnp.where(slot == 0, 0.0, tail[...]) + block


def begin_kernel(limit_ref, start_ref, full_ref, *quarters):
    slot = pl.program_id(0)
    value = masked(start_ref[0], limit_ref[slot])
    full_ref[0] = value
    put_quarter(slot, value, quarters)
    put_sums(slot, [value * value], quarters[0].at[pl.ds(quarters[0].shape[0] - TAIL, TAIL), :])


def heights(slots, blk):
    per = slots // PARTS * blk
    return [per + TAIL] + [per] * (PARTS - 1)


def whole_spec(shape):
    return pl.BlockSpec(shape, lambda s, *_: (0,) * len(shape))


def begin(limit, start):
    slots, blk, _ = start.shape
    sizes = heights(slots, blk)
    outs = pl.pallas_call(
        begin_kernel,
        out_shape=[jax.ShapeDtypeStruct(start.shape, jnp.float32)]
        + [jax.ShapeDtypeStruct((size, blk), jnp.float32) for size in sizes],
        grid_spec=pltpu.PrefetchScalarGridSpec(
            num_scalar_prefetch=1,
            grid=(slots,),
            in_specs=[pl.BlockSpec((1, blk, blk), lambda s, _: (s, 0, 0))],
            out_specs=[pl.BlockSpec((1, blk, blk), lambda s, _: (s, 0, 0))]
            + [whole_spec((size, blk)) for size in sizes],
        ),
    )(limit, start)
    return outs[0], outs[1:]


def apply_kernel(mode, rows_ref, limit_ref, coef_ref, *refs):
    pieces, refs = refs[: 2 * PARTS], refs[2 * PARTS :]
    left_ref, right_ref, refs = refs[0], refs[1], refs[2:]
    states, outs = refs[:mode], refs[mode:-3]
    blocks, inner, sems = refs[-3:]
    terms, _, blk, _ = left_ref.shape
    slot = pl.program_id(0)

    @pl.when(slot == 0)
    def _():
        copies = []
        at = 0
        for number, piece in enumerate(pieces):
            size = piece.shape[0]
            copies.append(
                pltpu.make_async_copy(piece, blocks.at[pl.ds(at, size), :], sems.at[number])
            )
            at += size
        for copy in copies:
            copy.start()
        for copy in copies:
            copy.wait()

    for term in range(terms):
        row = pl.multiple_of(rows_ref[slot, term], 8)
        first = jnp.concatenate(split(blocks[pl.ds(row, blk), :]), axis=1)
        value = folded(dot(first, right_factor(*split(right_ref[term, slot]))))
        inner[term * blk : (term + 1) * blk, :] = jnp.concatenate(split(value), axis=1)
    result = None
    for term in range(0, terms, 2):
        (high0, low0), (high1, low1) = (split(left_ref[index, slot]) for index in (term, term + 1))
        below = inner[term * blk : (term + 2) * blk, :]
        part = folded(dot(jnp.concatenate([high0, high1], axis=1), below))
        part = part + dot(jnp.concatenate([low0, low1], axis=1), below[:, :blk])
        result = part if result is None else result + part
    value = masked(result, limit_ref[slot])

    x0 = states[0][0] * coef_ref[0]
    if mode == 1:
        y0 = value * coef_ref[0]
        products = [x0 * y0]
        send = y0
    else:
        a0 = coef_ref[1]
        y0 = states[1][0]
        r1 = y0 - a0 * x0
        if mode == 2:
            z1 = value - a0 * y0
            products = [x0 * z1, r1 * y0, r1 * z1, r1 * r1]
            send = z1
        else:
            keep, turn, a1 = coef_ref[2], coef_ref[3], coef_ref[4]
            z1 = states[2][0]
            x1 = keep * x0 + turn * r1
            y1 = keep * y0 + turn * z1
            r2 = y1 - a1 * x1
            z2 = keep * (z1 + a0 * y0) + turn * value - a1 * y1
            products = [r2 * r2, r2 * z2]
            outs[0][0] = x1
            outs[1][0] = r2
            put_sums(slot, products, outs[2])
            return
    outs[0][0] = send
    put_quarter(slot, send, outs[1:])
    put_sums(slot, products, outs[1].at[pl.ds(outs[1].shape[0] - TAIL, TAIL), :])


def apply(rows, limit, coefs, pieces, left, right, states):
    mode = len(states)
    terms, slots, blk, _ = left.shape
    vector = jax.ShapeDtypeStruct((slots, blk, blk), jnp.float32)
    vector_spec = pl.BlockSpec((1, blk, blk), lambda s, *_: (s, 0, 0))
    if mode < 3:
        sizes = heights(slots, blk)
        out_shape = [vector] + [jax.ShapeDtypeStruct((size, blk), jnp.float32) for size in sizes]
        out_specs = [vector_spec] + [whole_spec((size, blk)) for size in sizes]
    else:
        out_shape = [vector, vector, jax.ShapeDtypeStruct((TAIL, blk), jnp.float32)]
        out_specs = [vector_spec, vector_spec, whole_spec((TAIL, blk))]
    total = sum(piece.shape[0] for piece in pieces)
    return pl.pallas_call(
        functools.partial(apply_kernel, mode),
        out_shape=out_shape,
        grid_spec=pltpu.PrefetchScalarGridSpec(
            num_scalar_prefetch=3,
            grid=(slots,),
            in_specs=[pl.BlockSpec(memory_space=pl.ANY)] * len(pieces)
            + [pl.BlockSpec(memory_space=pltpu.VMEM)] * 2
            + [vector_spec] * mode,
            out_specs=out_specs,
            scratch_shapes=[
                pltpu.VMEM((total, blk), jnp.float32),
                pltpu.VMEM((terms * blk, 2 * blk), jnp.bfloat16),
                pltpu.SemaphoreType.DMA((len(pieces),)),
            ],
        ),
        compiler_params=pltpu.CompilerParams(vmem_limit_bytes=20 * MIB),
        cost_estimate=pl.CostEstimate(
            flops=8 * terms * slots * blk**3, bytes_accessed=8 * left.size, transcendentals=0
        ),
    )(rows, limit, coefs, *pieces, left, right, *states)


def partner(index, move):
    axis, flip = move
    z, y = index // SIDE, index % SIDE
    return z * SIDE + (y ^ flip) if axis == "y" else (z ^ flip) * SIDE + y


def swap(value, move, count):
    return lax.ppermute(value, "sector", [(index, partner(index, move)) for index in range(count)])


def gather(quarters, count):
    held = list(quarters)
    for step in range(len(ORDERS[0])):
        came = [swap(value, order[step], count) for value, order in zip(held, ORDERS)]
        if step == len(ORDERS[0]) - 1:
            return [piece for pair in zip(held, came) for piece in pair]
        held = [jnp.concatenate(pair, axis=0) for pair in zip(held, came)]


def place_of(apart, flips):
    first, second = flips
    both = first ^ second
    return jnp.where(apart == first, 1, jnp.where(apart == second, 2, jnp.where(apart == both, 3, 0)))


def block_rows(source, owner, sdev, blk):
    device, slot = source // sdev, source % sdev
    apart = device ^ owner
    apart = {"z": apart // SIDE, "y": apart % SIDE}
    per = sdev // PARTS
    sizes = heights(sdev, blk)
    rows = jnp.zeros_like(source)
    base = 0
    for part, order in enumerate(ORDERS):
        (near, one), (_, two), (far, three), (_, four) = order
        unit = place_of(apart[near], (one, two)) + SIDE * place_of(apart[far], (three, four))
        here = base + unit * sizes[part] + (slot % per) * blk
        rows = jnp.where(slot // per == part, here, rows)
        base += SIDE * SIDE * sizes[part]
    return rows


def passed_along(value, axis, steps):
    count = lax.axis_size(axis)
    leading, last = (max(0, -steps), min(count, count - steps))
    return lax.ppermute(value, axis, [(source, source + steps) for source in range(leading, last)])


def mix(a, b2, rz):
    b = jnp.sqrt(b2)
    d = rz / b2
    lam = (a + d) / 2 - jnp.sqrt(((a - d) / 2) ** 2 + b2)
    q = lam - a
    n = jnp.sqrt(b2 + q * q)
    return lam, b / n, (q / b) / n


def body(left_env, right_env, site_block, start_vec, slot_sector, couple, dims, kept):
    lenv = left_env[0]
    renv = right_env[0]
    site = site_block[0]
    start = start_vec[0]
    sdev = start.shape[0]
    blk = start.shape[1]
    nsec = slot_sector.shape[0]
    devices = nsec // sdev
    owner = lax.axis_index("sector")
    slots = owner * sdev + jnp.arange(sdev, dtype=jnp.int32)
    sector_ids = jnp.take(slot_sector, slots)
    limit = dims[sector_ids] * kept[sector_ids]
    inverse = jnp.zeros((nsec,), jnp.int32).at[slot_sector].set(jnp.arange(nsec, dtype=jnp.int32))
    rows = block_rows(inverse[couple[sector_ids]], owner, sdev, blk)

    def totals(pieces, number):
        size = heights(sdev, blk)[0]
        tails = [piece.reshape(-1, size, blk)[:, size - TAIL : size - TAIL + number] for piece in pieces[:2]]
        found = jnp.sum(tails[0] + tails[1], axis=(0, 2))
        return [found[k] for k in range(number)]

    def coefs(*values):
        return jnp.stack(values + (jnp.float32(0),) * (8 - len(values)))

    updated = update(lenv, site)
    arrived = passed_along(updated, "chain", 1)
    luse = jnp.where(lax.axis_index("chain") == 0, lenv, arrived)
    luse = pltpu.with_memory_space_constraint(luse, pltpu.VMEM)
    ruse = pltpu.with_memory_space_constraint(renv, pltpu.VMEM)

    k0, quarters = begin(limit, start)
    pieces = gather(quarters, devices)
    (norm,) = totals(pieces, 1)
    scale = 1.0 / jnp.sqrt(norm + 1e-06)
    y0, *quarters = apply(rows, limit, coefs(scale), pieces, luse, ruse, [k0])
    pieces = gather(quarters, devices)
    (a0,) = totals(pieces, 1)
    z1, *quarters = apply(rows, limit, coefs(scale, a0), pieces, luse, ruse, [k0, y0])
    pieces = gather(quarters, devices)
    xz, ry, rz, rr = totals(pieces, 4)
    _, keep, turn = mix(a0, rr + 1e-06, rz)
    a1 = keep * keep * a0 + keep * turn * (xz + ry) + turn * turn * rz
    x1, r2, sums = apply(
        rows, limit, coefs(scale, a0, keep, turn, a1), pieces, luse, ruse, [k0, y0, z1]
    )
    for move in ORDERS[0]:
        sums = sums + swap(sums, move, devices)
    sums = jnp.sum(sums, axis=1)
    lam, keep, turn = mix(a1, sums[0] + 1e-06, sums[1])
    x2 = keep * x1 + turn * r2
    return (x2[None], updated[None], jnp.reshape(lam, (1,)))


def solution(mesh):
    placed = (
        P("chain", None, "sector", None, None),
        P("chain", None, "sector", None, None),
        P("chain", "sector", None, None),
        P("chain", "sector", None, None),
        P(),
        P(),
        P(),
        P(),
    )
    return jax.shard_map(
        body,
        mesh=mesh,
        in_specs=placed,
        out_specs=(
            P("chain", "sector", None, None),
            P("chain", None, "sector", None, None),
            P("chain"),
        ),
        check_vma=False,
    )
```

```python
import functools

import jax
import jax.numpy as jnp
from jax import lax
from jax.experimental import pallas as pl
from jax.experimental.pallas import tpu as pltpu
from jax.sharding import PartitionSpec as P

MIB = 1 << 20
TAIL = 8
PARTS = 4
SIDE = 4
PAIR = 2
AHEAD = 3
ORDERS = ((("y", 1), ("y", 3), ("z", 1), ("z", 3)), (("y", 3), ("y", 1), ("z", 3), ("z", 1)),
          (("z", 1), ("z", 3), ("y", 1), ("y", 3)), (("z", 3), ("z", 1), ("y", 3), ("y", 1)))


def split(value):
    high = value.astype(jnp.bfloat16)
    low = (value - high.astype(jnp.float32)).astype(jnp.bfloat16)
    return high, low


def dot(left, right):
    return jnp.dot(left, right, preferred_element_type=jnp.float32)


def right_factor(high, low):
    top = jnp.concatenate([high, low], axis=1)
    bottom = jnp.concatenate([high, jnp.zeros_like(low)], axis=1)
    return jnp.concatenate([top, bottom], axis=0)


def folded(value):
    half = value.shape[1] // 2
    return value[:, :half] + value[:, half:]


def update_kernel(left_ref, site_ref, out_ref, inner, outer):
    terms, slots, blk, _ = left_ref.shape

    @pl.when(pl.program_id(0) == 0)
    def _():
        for slot in range(slots):
            site = site_ref[slot]
            inner[slot] = right_factor(*split(site))
            high, low = split(site.T)
            outer[slot] = jnp.concatenate([high, low, high], axis=1)

    for slot in range(slots):
        first = [jnp.concatenate(split(left_ref[index, slot]), axis=1) for index in range(terms)]
        half = folded(dot(jnp.concatenate(first, axis=0), inner[slot]))
        high, low = split(half)
        columns = []
        for index in range(terms):
            rows = slice(index * blk, (index + 1) * blk)
            columns.append(jnp.concatenate([high[rows], high[rows], low[rows]], axis=0))
        both = dot(outer[slot], jnp.concatenate(columns, axis=1))
        for index in range(terms):
            value = both[:, index * blk : (index + 1) * blk]
            out_ref[index, slot] = value


def update(left, site, at, some):
    _, slots, blk, _ = left.shape
    pair = PAIR
    return pl.pallas_call(
        update_kernel,
        out_shape=jax.ShapeDtypeStruct((some, slots, blk, blk), jnp.float32),
        grid=(some // pair,),
        in_specs=[
            pl.BlockSpec((pair, slots, blk, blk), lambda t: (at // pair + t, 0, 0, 0)),
            pl.BlockSpec((slots, blk, blk), lambda t: (0, 0, 0)),
        ],
        out_specs=pl.BlockSpec((pair, slots, blk, blk), lambda t: (t, 0, 0, 0)),
        scratch_shapes=[
            pltpu.VMEM((slots, 2 * blk, 2 * blk), jnp.bfloat16),
            pltpu.VMEM((slots, blk, 3 * blk), jnp.bfloat16),
        ],
        compiler_params=pltpu.CompilerParams(vmem_limit_bytes=12 * MIB),
        cost_estimate=pl.CostEstimate(
            flops=8 * some * slots * blk**3,
            bytes_accessed=8 * some * slots * blk * blk,
            transcendentals=0,
        ),
    )(left, site)


def join_kernel(starts, *refs):
    parts, out_ref = refs[: len(starts) - 1], refs[-1]
    step = pl.program_id(0)
    for part, start, end in zip(parts, starts, starts[1:]):
        @pl.when((step >= start) & (step < end))
        def _(part=part):
            out_ref[...] = part[...]


def join(parts, after):
    shape = parts[0].shape[1:]
    starts = [0]
    for part in parts:
        starts.append(starts[-1] + part.shape[0] // PAIR)
    specs = [
        pl.BlockSpec(
            (PAIR,) + shape, lambda t, start=start, end=end: (jnp.clip(t - start, 0, end - start - 1), 0, 0, 0)
        )
        for start, end in zip(starts, starts[1:])
    ]
    return pl.pallas_call(
        functools.partial(join_kernel, starts),
        out_shape=jax.ShapeDtypeStruct((PAIR * starts[-1],) + shape, jnp.float32),
        grid=(starts[-1],),
        in_specs=specs + [pl.BlockSpec(memory_space=pl.ANY)],
        out_specs=pl.BlockSpec((PAIR,) + shape, lambda t: (t, 0, 0, 0)),
        compiler_params=pltpu.CompilerParams(vmem_limit_bytes=12 * MIB),
        cost_estimate=pl.CostEstimate(
            flops=0, bytes_accessed=8 * sum(part.size for part in parts), transcendentals=0
        ),
    )(*parts, after)


def masked(value, limit):
    rows = lax.broadcasted_iota(jnp.int32, value.shape, 0)
    columns = lax.broadcasted_iota(jnp.int32, value.shape, 1)
    return jnp.where(jnp.maximum(rows, columns) < limit, value, 0.0)


def put_quarter(slot, value, quarters):
    blk = value.shape[0]
    per = pl.num_programs(0) // PARTS
    at = pl.ds(pl.multiple_of((slot % per) * blk, blk), blk)
    for part, quarter in enumerate(quarters):
        @pl.when(slot // per == part)
        def _(quarter=quarter):
            quarter[at, :] = value


def tail_of(products):
    rows = [jnp.sum(product, axis=0, keepdims=True) for product in products]
    rows.append(jnp.zeros((TAIL - len(rows), rows[0].shape[1]), jnp.float32))
    return jnp.concatenate(rows, axis=0)


def put_sums(slot, products, tail):
    tail[...] = jnp.where(slot == 0, 0.0, tail[...]) + tail_of(products)


def begin_kernel(owner_ref, sector_ref, dims_ref, kept_ref, start_ref, full_ref, limit_ref, packed_ref):
    slots, blk, _ = start_ref.shape
    total = jnp.zeros((blk, blk), jnp.float32)
    for slot in range(slots):
        sector = sector_ref[owner_ref[0] * slots + slot]
        limit = dims_ref[sector] * kept_ref[sector]
        limit_ref[slot] = limit
        value = masked(start_ref[slot], limit)
        full_ref[slot] = value
        packed_ref[slot * blk : (slot + 1) * blk, :] = value
        total = total + value * value
    packed_ref[slots * blk :, :] = tail_of([total])


def heights(slots, blk):
    per = slots // PARTS * blk
    return [per + TAIL] + [per] * (PARTS - 1)


def whole_spec(shape):
    return pl.BlockSpec(shape, lambda s, *_: (0,) * len(shape))


def begin(owner, slot_sector, dims, kept, start):
    slots, blk, _ = start.shape
    vmem = pl.BlockSpec(memory_space=pltpu.VMEM)
    smem = pl.BlockSpec(memory_space=pltpu.SMEM)
    return pl.pallas_call(
        begin_kernel,
        out_shape=[
            jax.ShapeDtypeStruct(start.shape, jnp.float32),
            jax.ShapeDtypeStruct((slots,), jnp.int32),
        ]
        + [jax.ShapeDtypeStruct((slots * blk + TAIL, blk), jnp.float32)],
        in_specs=[smem] * 4 + [vmem],
        out_specs=[vmem, smem, vmem],
        compiler_params=pltpu.CompilerParams(vmem_limit_bytes=4 * MIB),
    )(owner, slot_sector, dims, kept, start)


def start_fetch(slot, which, lefts, right, left_copy, right_copy, sems):
    own, near, far = lefts
    pltpu.make_async_copy(right.at[:, slot], right_copy.at[:, slot], sems.at[0, slot]).start()
    for number in range(3):
        @pl.when(which == number)
        def _(number=number):
            at = 0
            for part, ref in enumerate((near, far)[number - 1] if number else near):
                here = slice(at, at + ref.shape[0])
                source = ref.at[:, slot] if number else own.at[here, slot]
                at += ref.shape[0]
                pltpu.make_async_copy(
                    source, left_copy.at[here, slot], sems.at[1 + part, slot]
                ).start()


def wait_fetch(slot, lefts, right, left_copy, right_copy, sems):
    pltpu.make_async_copy(right.at[:, slot], right_copy.at[:, slot], sems.at[0, slot]).wait()
    own, near, _ = lefts
    at = 0
    for part, ref in enumerate(near):
        here = slice(at, at + ref.shape[0])
        pltpu.make_async_copy(
            own.at[here, slot], left_copy.at[here, slot], sems.at[1 + part, slot]
        ).wait()
        at += ref.shape[0]


def mix(a, b2, rz):
    b = jnp.sqrt(b2)
    d = rz / b2
    lam = (a + d) / 2 - jnp.sqrt(((a - d) / 2) ** 2 + b2)
    q = lam - a
    n = jnp.sqrt(b2 + q * q)
    return lam, b / n, (q / b) / n


def next_coefs(mode, known, sums):
    row = lambda value, k: value[k : k + 1, :]
    total = jnp.broadcast_to(jnp.sum(sums, axis=1, keepdims=True), sums.shape)
    rows = [row(known, k) for k in range(5)]
    if mode == 1:
        rows[0] = 1.0 / jnp.sqrt(row(total, 0) + 1e-06)
    elif mode == 2:
        rows[1] = row(total, 0)
    else:
        xz, ry, rz, rr = (row(total, k) for k in range(4))
        a0 = rows[1]
        _, keep, turn = mix(a0, rr + 1e-06, rz)
        rows[2:4] = keep, turn
        rows[4] = keep * keep * a0 + keep * turn * (xz + ry) + turn * turn * rz
    rows.append(jnp.zeros((TAIL - len(rows), sums.shape[1]), jnp.float32))
    return jnp.concatenate(rows, axis=0)


def apply_kernel(mode, counts, tails, rows_ref, limit_ref, which_ref, *refs):
    refs = list(refs)
    pieces, own, near, far = ([refs.pop(0) for _ in range(count)] for count in counts)
    lefts = own[0], near, far
    right, known_ref = refs.pop(0), refs.pop(0)
    states, outs = refs[:mode], refs[mode:-6]
    blocks, left_copy, right_copy, inner, sems, piece_sems = refs[-6:]
    terms, _, blk, _ = left_copy.shape
    slot = pl.program_id(0)
    coef_ref = outs[0]
    outs = outs[1:]

    @pl.when(slot == 0)
    def _():
        copies = []
        at = 0
        for number, piece in enumerate(pieces):
            size = piece.shape[0]
            copies.append(
                pltpu.make_async_copy(piece, blocks.at[pl.ds(at, size), :], piece_sems.at[number])
            )
            at += size
        for copy in copies:
            copy.start()
        for early in range(AHEAD):
            start_fetch(early, which_ref[0], lefts, right, left_copy, right_copy, sems)
        for copy in copies:
            copy.wait()
        sums = blocks[tails[0] : tails[0] + TAIL, :]
        for tail in tails[1:]:
            sums = sums + blocks[tail : tail + TAIL, :]
        coef_ref[...] = next_coefs(mode, known_ref[...], sums)

    @pl.when(slot + AHEAD < pl.num_programs(0))
    def _():
        start_fetch(slot + AHEAD, which_ref[0], lefts, right, left_copy, right_copy, sems)

    wait_fetch(slot, lefts, right, left_copy, right_copy, sems)
    for term in range(terms):
        row = pl.multiple_of(rows_ref[slot, term], 8)
        first = jnp.concatenate(split(blocks[pl.ds(row, blk), :]), axis=1)
        value = folded(dot(first, right_factor(*split(right_copy[term, slot]))))
        inner[term * blk : (term + 1) * blk, :] = jnp.concatenate(split(value), axis=1)
    result = None
    for term in range(0, terms, 2):
        (high0, low0), (high1, low1) = (
            split(left_copy[index, slot]) for index in (term, term + 1)
        )
        below = inner[term * blk : (term + 2) * blk, :]
        part = folded(dot(jnp.concatenate([high0, high1], axis=1), below))
        part = part + dot(jnp.concatenate([low0, low1], axis=1), below[:, :blk])
        result = part if result is None else result + part
    value = masked(result, limit_ref[slot])

    scale, a0, keep, turn, a1 = (coef_ref[k : k + 1, :] for k in range(5))
    x0 = states[0][0] * scale
    if mode == 1:
        y0 = value * scale
        products = [x0 * y0]
        send = y0
    else:
        y0 = states[1][0]
        r1 = y0 - a0 * x0
        if mode == 2:
            z1 = value - a0 * y0
            products = [x0 * z1, r1 * y0, r1 * z1, r1 * r1]
            send = z1
        else:
            z1 = states[2][0]
            x1 = keep * x0 + turn * r1
            y1 = keep * y0 + turn * z1
            r2 = y1 - a1 * x1
            z2 = keep * (z1 + a0 * y0) + turn * value - a1 * y1
            outs[0][0] = x1
            outs[1][0] = r2
            put_sums(slot, [r2 * r2, r2 * z2], outs[2])
            return
    outs[0][0] = send
    put_quarter(slot, send, outs[1:])
    put_sums(slot, products, outs[1].at[pl.ds(outs[1].shape[0] - TAIL, TAIL), :])


def apply(rows, limit, which, tails, pieces, lefts, right, known, states):
    mode = len(states)
    terms, slots, blk, _ = right.shape
    vector = jax.ShapeDtypeStruct((slots, blk, blk), jnp.float32)
    vector_spec = pl.BlockSpec((1, blk, blk), lambda s, *_: (s, 0, 0))
    few = jax.ShapeDtypeStruct((TAIL, blk), jnp.float32)
    few_spec = whole_spec((TAIL, blk))
    if mode < 3:
        sizes = heights(slots, blk)
        out_shape = [few, vector]
        out_shape += [jax.ShapeDtypeStruct((size, blk), jnp.float32) for size in sizes]
        out_specs = [few_spec, vector_spec] + [whole_spec((size, blk)) for size in sizes]
    else:
        out_shape = [few, vector, vector, few]
        out_specs = [few_spec, vector_spec, vector_spec, few_spec]
    total = sum(piece.shape[0] for piece in pieces)
    own, near, far = lefts
    counts = (len(pieces), 1, len(near), len(far))
    return pl.pallas_call(
        functools.partial(apply_kernel, mode, counts, tails),
        out_shape=out_shape,
        grid_spec=pltpu.PrefetchScalarGridSpec(
            num_scalar_prefetch=3,
            grid=(slots,),
            in_specs=[pl.BlockSpec(memory_space=pl.ANY)] * (sum(counts) + 1)
            + [few_spec]
            + [vector_spec] * mode,
            out_specs=out_specs,
            scratch_shapes=[
                pltpu.VMEM((total, blk), jnp.float32),
                pltpu.VMEM(right.shape, jnp.float32),
                pltpu.VMEM(right.shape, jnp.float32),
                pltpu.VMEM((terms * blk, 2 * blk), jnp.bfloat16),
                pltpu.SemaphoreType.DMA((1 + len(near), slots)),
                pltpu.SemaphoreType.DMA((len(pieces),)),
            ],
        ),
        compiler_params=pltpu.CompilerParams(vmem_limit_bytes=30 * MIB),
        cost_estimate=pl.CostEstimate(
            flops=8 * terms * slots * blk**3, bytes_accessed=12 * right.size, transcendentals=0
        ),
    )(rows, limit, which, *pieces, own, *near, *far, right, known, *states)


def finish_kernel(sums_ref, coef_ref, one_ref, other_ref, out_ref, energy_ref):
    sums = jnp.sum(sums_ref[...], axis=0)
    total = jnp.broadcast_to(jnp.sum(sums, axis=1, keepdims=True), sums.shape)
    lam, keep, turn = mix(coef_ref[4:5, :], total[0:1, :] + 1e-06, total[1:2, :])
    energy_ref[...] = jnp.broadcast_to(lam, energy_ref.shape)
    for slot in range(one_ref.shape[0]):
        out_ref[slot] = keep * one_ref[slot] + turn * other_ref[slot]


def finish(sums, coefs, one, other):
    return pl.pallas_call(
        finish_kernel,
        out_shape=[
            jax.ShapeDtypeStruct(one.shape, jnp.float32),
            jax.ShapeDtypeStruct(coefs.shape, jnp.float32),
        ],
        compiler_params=pltpu.CompilerParams(vmem_limit_bytes=4 * MIB),
    )(sums, coefs, one, other)


def partner(index, move):
    axis, flip = move
    z, y = index // SIDE, index % SIDE
    return z * SIDE + (y ^ flip) if axis == "y" else (z ^ flip) * SIDE + y


def swap(value, move, count):
    return lax.ppermute(value, "sector", [(index, partner(index, move)) for index in range(count)])


def gather(quarters, count):
    held = list(quarters)
    for step in range(len(ORDERS[0])):
        last = step == len(ORDERS[0]) - 1
        came = [swap(value, order[step], count) for value, order in zip(held, ORDERS)]
        if last:
            return [piece for pair in zip(held, came) for piece in pair]
        held = [jnp.concatenate(pair, axis=0) for pair in zip(held, came)]


def place_of(apart, flips):
    first, second = flips
    both = first ^ second
    return jnp.where(apart == first, 1, jnp.where(apart == second, 2, jnp.where(apart == both, 3, 0)))


def block_rows(source, owner, sdev, blk):
    device, slot = source // sdev, source % sdev
    apart = device ^ owner
    apart = {"z": apart // SIDE, "y": apart % SIDE}
    per = sdev // PARTS
    sizes = heights(sdev, blk)
    rows = jnp.zeros_like(source)
    base = 0
    for part, order in enumerate(ORDERS):
        (near, one), (_, two), (far, three), (_, four) = order
        unit = place_of(apart[near], (one, two)) + SIDE * place_of(apart[far], (three, four))
        here = base + unit * sizes[part] + (slot % per) * blk
        rows = jnp.where(slot // per == part, here, rows)
        base += SIDE * SIDE * sizes[part]
    return rows


def to_next(value):
    count = lax.axis_size("chain")
    return lax.ppermute(value, "chain", [(source, source + 1) for source in range(count - 1)])


def to_next_round(value):
    count = lax.axis_size("chain")
    inside = [(source, source + 1) for source in range(0, count, 2)]
    places = [(source - 3) % count for source in range(1, count - 1, 2)]
    pairs = inside + list(zip(range(1, count - 1, 2), places))
    near = value = lax.ppermute(value, "chain", pairs)
    for _ in range(count // 2 - 2):
        pairs = [(place, (place - 2) % count) for place in places]
        value = lax.ppermute(value, "chain", pairs)
        places = [place for _, place in pairs]
    return near, value


def body(left_env, right_env, site_block, start_vec, slot_sector, couple, dims, kept):
    lenv = left_env[0]
    renv = right_env[0]
    site = site_block[0]
    start = start_vec[0]
    sdev = start.shape[0]
    blk = start.shape[1]
    nsec = slot_sector.shape[0]
    devices = nsec // sdev
    owner = lax.axis_index("sector")
    slots = owner * sdev + jnp.arange(sdev, dtype=jnp.int32)
    sector_ids = jnp.take(slot_sector, slots)
    inverse = jnp.zeros((nsec,), jnp.int32).at[slot_sector].set(jnp.arange(nsec, dtype=jnp.int32))
    source = inverse[couple[sector_ids]]
    rows = block_rows(source, owner, sdev, blk)

    chain = lax.axis_index("chain")
    which = jnp.where(chain == 0, 0, jnp.where(chain % 2 == 1, 1, 2)).astype(jnp.int32).reshape(1)
    terms = lenv.shape[0]

    def in_hbm(value):
        return pltpu.with_memory_space_constraint(value, pltpu.HBM)

    k0, limit, packed = begin(
        owner.astype(jnp.int32).reshape(1),
        *(in_hbm(value) for value in (slot_sector, dims, kept, start)),
    )
    site, k0 = lax.optimization_barrier((site, k0))
    lenv = in_hbm(lenv)
    whole = lax.all_gather(packed, "sector", axis=0, tiled=True)
    some = terms // 8
    sizes = [terms // 2, terms - terms // 2 - 2 * some, some, some]
    built = {}
    for number in (0, 2, 3, 1):
        part = update(lenv, site, sum(sizes[:number]), sizes[number])
        if number < 2:
            near = far = to_next(part)
        else:
            near, far = to_next_round(part)
        built[number] = tuple(in_hbm(value) for value in (part, near, far))
    parts, nears, fars = ([built[number][k] for number in range(len(sizes))] for k in range(3))
    lefts = lenv, nears, fars
    right = in_hbm(renv)

    height = sdev * blk + TAIL
    tails = [device * height + height - TAIL for device in range(devices)]
    first_rows = (source // sdev) * height + (source % sdev) * blk
    known = jnp.zeros((TAIL, blk), jnp.float32)
    known, y0, *quarters = apply(
        first_rows, limit, which, tails, [whole], lefts, right, known, [k0]
    )
    height = heights(sdev, blk)[0]
    tails = [unit * height + height - TAIL for unit in range(SIDE * SIDE)]
    pieces = gather(quarters, devices)
    updated = join(parts, pieces[0])
    pieces, updated = lax.optimization_barrier((pieces, updated))
    known, z1, *quarters = apply(rows, limit, which, tails, pieces, lefts, right, known, [k0, y0])
    pieces = gather(quarters, devices)
    known, x1, r2, sums = apply(
        rows, limit, which, tails, pieces, lefts, right, known, [k0, y0, z1]
    )
    for axis in ("y", "z"):
        others = [swap(sums, (axis, flip), devices) for flip in range(1, SIDE)]
        if axis == "y":
            sums = (sums + others[0]) + (others[1] + others[2])
    x2, energy = finish(jnp.stack([sums] + others), known, x1, r2)
    return (x2[None], updated[None], energy[0, :1])


def solution(mesh):
    placed = (
        P("chain", None, "sector", None, None),
        P("chain", None, "sector", None, None),
        P("chain", "sector", None, None),
        P("chain", "sector", None, None),
        P(),
        P(),
        P(),
        P(),
    )
    return jax.shard_map(
        body,
        mesh=mesh,
        in_specs=placed,
        out_specs=(
            P("chain", "sector", None, None),
            P("chain", None, "sector", None, None),
            P("chain"),
        ),
        check_vma=False,
    )
```

```python
import functools

import jax
import jax.numpy as jnp
from jax import lax
from jax.experimental import pallas as pl
from jax.experimental.pallas import tpu as pltpu
from jax.sharding import PartitionSpec as P

MIB = 1 << 20
TAIL = 8
PARTS = 4
SIDE = 4
PAIR = 2
AHEAD = 3
ORDERS = ((("y", 1), ("y", 3), ("z", 1), ("z", 3)), (("y", 3), ("y", 1), ("z", 3), ("z", 1)),
          (("z", 1), ("z", 3), ("y", 1), ("y", 3)), (("z", 3), ("z", 1), ("y", 3), ("y", 1)))


def split(value):
    high = value.astype(jnp.bfloat16)
    low = (value - high.astype(jnp.float32)).astype(jnp.bfloat16)
    return high, low


def dot(left, right):
    return jnp.dot(left, right, preferred_element_type=jnp.float32)


def right_factor(high, low):
    top = jnp.concatenate([high, low], axis=1)
    bottom = jnp.concatenate([high, jnp.zeros_like(low)], axis=1)
    return jnp.concatenate([top, bottom], axis=0)


def folded(value):
    half = value.shape[1] // 2
    return value[:, :half] + value[:, half:]


def update_kernel(left_ref, site_ref, out_ref, inner, outer):
    terms, slots, blk, _ = left_ref.shape

    @pl.when(pl.program_id(0) == 0)
    def _():
        for slot in range(slots):
            site = site_ref[slot]
            inner[slot] = right_factor(*split(site))
            high, low = split(site.T)
            outer[slot] = jnp.concatenate([high, low, high], axis=1)

    for slot in range(slots):
        first = [jnp.concatenate(split(left_ref[index, slot]), axis=1) for index in range(terms)]
        half = folded(dot(jnp.concatenate(first, axis=0), inner[slot]))
        high, low = split(half)
        columns = []
        for index in range(terms):
            rows = slice(index * blk, (index + 1) * blk)
            columns.append(jnp.concatenate([high[rows], high[rows], low[rows]], axis=0))
        both = dot(outer[slot], jnp.concatenate(columns, axis=1))
        for index in range(terms):
            value = both[:, index * blk : (index + 1) * blk]
            out_ref[index, slot] = value


def update(left, site, at, some):
    _, slots, blk, _ = left.shape
    pair = PAIR
    return pl.pallas_call(
        update_kernel,
        out_shape=jax.ShapeDtypeStruct((some, slots, blk, blk), jnp.float32),
        grid=(some // pair,),
        in_specs=[
            pl.BlockSpec((pair, slots, blk, blk), lambda t: (at // pair + t, 0, 0, 0)),
            pl.BlockSpec((slots, blk, blk), lambda t: (0, 0, 0)),
        ],
        out_specs=pl.BlockSpec((pair, slots, blk, blk), lambda t: (t, 0, 0, 0)),
        scratch_shapes=[
            pltpu.VMEM((slots, 2 * blk, 2 * blk), jnp.bfloat16),
            pltpu.VMEM((slots, blk, 3 * blk), jnp.bfloat16),
        ],
        compiler_params=pltpu.CompilerParams(vmem_limit_bytes=12 * MIB),
        cost_estimate=pl.CostEstimate(
            flops=8 * some * slots * blk**3,
            bytes_accessed=8 * some * slots * blk * blk,
            transcendentals=0,
        ),
    )(left, site)


def join_kernel(starts, *refs):
    parts, out_ref = refs[: len(starts) - 1], refs[-1]
    step = pl.program_id(0)
    for part, start, end in zip(parts, starts, starts[1:]):
        @pl.when((step >= start) & (step < end))
        def _(part=part):
            out_ref[...] = part[...]


def join(parts, after):
    shape = parts[0].shape[1:]
    starts = [0]
    for part in parts:
        starts.append(starts[-1] + part.shape[0] // PAIR)
    specs = [
        pl.BlockSpec(
            (PAIR,) + shape, lambda t, start=start, end=end: (jnp.clip(t - start, 0, end - start - 1), 0, 0, 0)
        )
        for start, end in zip(starts, starts[1:])
    ]
    return pl.pallas_call(
        functools.partial(join_kernel, starts),
        out_shape=jax.ShapeDtypeStruct((PAIR * starts[-1],) + shape, jnp.float32),
        grid=(starts[-1],),
        in_specs=specs + [pl.BlockSpec(memory_space=pl.ANY)],
        out_specs=pl.BlockSpec((PAIR,) + shape, lambda t: (t, 0, 0, 0)),
        compiler_params=pltpu.CompilerParams(vmem_limit_bytes=12 * MIB),
        cost_estimate=pl.CostEstimate(
            flops=0, bytes_accessed=8 * sum(part.size for part in parts), transcendentals=0
        ),
    )(*parts, after)


def masked(value, limit):
    rows = lax.broadcasted_iota(jnp.int32, value.shape, 0)
    columns = lax.broadcasted_iota(jnp.int32, value.shape, 1)
    return jnp.where(jnp.maximum(rows, columns) < limit, value, 0.0)


def put_quarter(slot, value, quarters):
    blk = value.shape[0]
    per = pl.num_programs(0) // PARTS
    at = pl.ds(pl.multiple_of((slot % per) * blk, blk), blk)
    for part, quarter in enumerate(quarters):
        @pl.when(slot // per == part)
        def _(quarter=quarter):
            quarter[at, :] = value


def tail_of(products):
    rows = [jnp.sum(product, axis=0, keepdims=True) for product in products]
    rows.append(jnp.zeros((TAIL - len(rows), rows[0].shape[1]), jnp.float32))
    return jnp.concatenate(rows, axis=0)


def put_sums(slot, products, tail):
    tail[...] = jnp.where(slot == 0, 0.0, tail[...]) + tail_of(products)


def begin_kernel(owner_ref, sector_ref, dims_ref, kept_ref, start_ref, full_ref, limit_ref, packed_ref):
    slots, blk, _ = start_ref.shape
    total = jnp.zeros((blk, blk), jnp.float32)
    for slot in range(slots):
        sector = sector_ref[owner_ref[0] * slots + slot]
        limit = dims_ref[sector] * kept_ref[sector]
        limit_ref[slot] = limit
        value = masked(start_ref[slot], limit)
        full_ref[slot] = value
        packed_ref[slot * blk : (slot + 1) * blk, :] = value
        total = total + value * value
    packed_ref[slots * blk :, :] = tail_of([total])


def heights(slots, blk):
    per = slots // PARTS * blk
    return [per + TAIL] + [per] * (PARTS - 1)


def whole_spec(shape):
    return pl.BlockSpec(shape, lambda s, *_: (0,) * len(shape))


def begin(owner, slot_sector, dims, kept, start):
    slots, blk, _ = start.shape
    vmem = pl.BlockSpec(memory_space=pltpu.VMEM)
    smem = pl.BlockSpec(memory_space=pltpu.SMEM)
    return pl.pallas_call(
        begin_kernel,
        out_shape=[
            jax.ShapeDtypeStruct(start.shape, jnp.float32),
            jax.ShapeDtypeStruct((slots,), jnp.int32),
        ]
        + [jax.ShapeDtypeStruct((slots * blk + TAIL, blk), jnp.float32)],
        in_specs=[smem] * 4 + [vmem],
        out_specs=[vmem, smem, vmem],
        compiler_params=pltpu.CompilerParams(vmem_limit_bytes=4 * MIB),
    )(owner, slot_sector, dims, kept, start)


def start_fetch(slot, which, lefts, right, left_copy, right_copy, sems):
    own, near, far = lefts
    pltpu.make_async_copy(right.at[:, slot], right_copy.at[:, slot], sems.at[0, slot]).start()
    for number in range(3):
        @pl.when(which == number)
        def _(number=number):
            at = 0
            for part, ref in enumerate((near, far)[number - 1] if number else near):
                here = slice(at, at + ref.shape[0])
                source = ref.at[:, slot] if number else own.at[here, slot]
                at += ref.shape[0]
                pltpu.make_async_copy(
                    source, left_copy.at[here, slot], sems.at[1 + part, slot]
                ).start()


def wait_fetch(slot, lefts, right, left_copy, right_copy, sems):
    pltpu.make_async_copy(right.at[:, slot], right_copy.at[:, slot], sems.at[0, slot]).wait()
    own, near, _ = lefts
    at = 0
    for part, ref in enumerate(near):
        here = slice(at, at + ref.shape[0])
        pltpu.make_async_copy(
            own.at[here, slot], left_copy.at[here, slot], sems.at[1 + part, slot]
        ).wait()
        at += ref.shape[0]


def mix(a, b2, rz):
    b = jnp.sqrt(b2)
    d = rz / b2
    lam = (a + d) / 2 - jnp.sqrt(((a - d) / 2) ** 2 + b2)
    q = lam - a
    n = jnp.sqrt(b2 + q * q)
    return lam, b / n, (q / b) / n


def next_coefs(mode, known, sums):
    row = lambda value, k: value[k : k + 1, :]
    total = jnp.broadcast_to(jnp.sum(sums, axis=1, keepdims=True), sums.shape)
    rows = [row(known, k) for k in range(5)]
    if mode == 1:
        rows[0] = 1.0 / jnp.sqrt(row(total, 0) + 1e-06)
    elif mode == 2:
        rows[1] = row(total, 0)
    else:
        xz, ry, rz, rr = (row(total, k) for k in range(4))
        a0 = rows[1]
        _, keep, turn = mix(a0, rr + 1e-06, rz)
        rows[2:4] = keep, turn
        rows[4] = keep * keep * a0 + keep * turn * (xz + ry) + turn * turn * rz
    rows.append(jnp.zeros((TAIL - len(rows), sums.shape[1]), jnp.float32))
    return jnp.concatenate(rows, axis=0)


def apply_kernel(mode, counts, tails, rows_ref, limit_ref, which_ref, *refs):
    refs = list(refs)
    whole, pieces, own, near, far = ([refs.pop(0) for _ in range(count)] for count in counts)
    whole = whole[0]
    split_row = whole.shape[0]
    lefts = own[0], near, far
    right, known_ref = refs.pop(0), refs.pop(0)
    states, outs = refs[:mode], refs[mode:-6]
    blocks, left_copy, right_copy, inner, sems, piece_sems = refs[-6:]
    terms, _, blk, _ = left_copy.shape
    slot = pl.program_id(0)
    coef_ref = outs[0]
    outs = outs[1:]

    def rows_of(row, number):
        if not pieces:
            return whole[pl.ds(row, number), :]
        early = whole[pl.ds(pl.multiple_of(jnp.minimum(row, split_row - number), 8), number), :]
        late = blocks[pl.ds(pl.multiple_of(jnp.maximum(row - split_row, 0), 8), number), :]
        return jnp.where(row < split_row, early, late)

    @pl.when(slot == 0)
    def _():
        copies = []
        at = 0
        for number, piece in enumerate(pieces):
            size = piece.shape[0]
            copies.append(
                pltpu.make_async_copy(piece, blocks.at[pl.ds(at, size), :], piece_sems.at[number])
            )
            at += size
        for copy in copies:
            copy.start()
        for early in range(AHEAD):
            start_fetch(early, which_ref[0], lefts, right, left_copy, right_copy, sems)
        for copy in copies:
            copy.wait()
        sums = None
        for tail in tails:
            source, at = (whole, tail) if tail < split_row else (blocks, tail - split_row)
            part = source[at : at + TAIL, :]
            sums = part if sums is None else sums + part
        coef_ref[...] = next_coefs(mode, known_ref[...], sums)

    @pl.when(slot + AHEAD < pl.num_programs(0))
    def _():
        start_fetch(slot + AHEAD, which_ref[0], lefts, right, left_copy, right_copy, sems)

    wait_fetch(slot, lefts, right, left_copy, right_copy, sems)
    for term in range(terms):
        row = pl.multiple_of(rows_ref[slot, term], 8)
        first = jnp.concatenate(split(rows_of(row, blk)), axis=1)
        value = folded(dot(first, right_factor(*split(right_copy[term, slot]))))
        inner[term * blk : (term + 1) * blk, :] = jnp.concatenate(split(value), axis=1)
    result = None
    for term in range(0, terms, 2):
        (high0, low0), (high1, low1) = (
            split(left_copy[index, slot]) for index in (term, term + 1)
        )
        below = inner[term * blk : (term + 2) * blk, :]
        part = folded(dot(jnp.concatenate([high0, high1], axis=1), below))
        part = part + dot(jnp.concatenate([low0, low1], axis=1), below[:, :blk])
        result = part if result is None else result + part
    value = masked(result, limit_ref[slot])

    scale, a0, keep, turn, a1 = (coef_ref[k : k + 1, :] for k in range(5))
    x0 = states[0][0] * scale
    if mode == 1:
        y0 = value * scale
        products = [x0 * y0]
        send = y0
    else:
        y0 = states[1][0]
        r1 = y0 - a0 * x0
        if mode == 2:
            z1 = value - a0 * y0
            products = [x0 * z1, r1 * y0, r1 * z1, r1 * r1]
            send = z1
        else:
            z1 = states[2][0]
            x1 = keep * x0 + turn * r1
            y1 = keep * y0 + turn * z1
            r2 = y1 - a1 * x1
            z2 = keep * (z1 + a0 * y0) + turn * value - a1 * y1
            outs[0][0] = x1
            outs[1][0] = r2
            put_sums(slot, [r2 * r2, r2 * z2], outs[2])
            return
    outs[0][0] = send
    put_quarter(slot, send, outs[1:])
    put_sums(slot, products, outs[1].at[pl.ds(outs[1].shape[0] - TAIL, TAIL), :])


def apply(rows, limit, which, tails, whole, pieces, lefts, right, known, states):
    mode = len(states)
    terms, slots, blk, _ = right.shape
    vector = jax.ShapeDtypeStruct((slots, blk, blk), jnp.float32)
    vector_spec = pl.BlockSpec((1, blk, blk), lambda s, *_: (s, 0, 0))
    few = jax.ShapeDtypeStruct((TAIL, blk), jnp.float32)
    few_spec = whole_spec((TAIL, blk))
    if mode < 3:
        sizes = heights(slots, blk)
        out_shape = [few, vector]
        out_shape += [jax.ShapeDtypeStruct((size, blk), jnp.float32) for size in sizes]
        out_specs = [few_spec, vector_spec] + [whole_spec((size, blk)) for size in sizes]
    else:
        out_shape = [few, vector, vector, few]
        out_specs = [few_spec, vector_spec, vector_spec, few_spec]
    total = sum(piece.shape[0] for piece in pieces) or TAIL
    own, near, far = lefts
    counts = (1, len(pieces), 1, len(near), len(far))
    return pl.pallas_call(
        functools.partial(apply_kernel, mode, counts, tails),
        out_shape=out_shape,
        grid_spec=pltpu.PrefetchScalarGridSpec(
            num_scalar_prefetch=3,
            grid=(slots,),
            in_specs=[pl.BlockSpec(memory_space=pltpu.VMEM)]
            + [pl.BlockSpec(memory_space=pl.ANY)] * sum(counts)
            + [few_spec]
            + [vector_spec] * mode,
            out_specs=out_specs,
            scratch_shapes=[
                pltpu.VMEM((total, blk), jnp.float32),
                pltpu.VMEM(right.shape, jnp.float32),
                pltpu.VMEM(right.shape, jnp.float32),
                pltpu.VMEM((terms * blk, 2 * blk), jnp.bfloat16),
                pltpu.SemaphoreType.DMA((1 + len(near), slots)),
                pltpu.SemaphoreType.DMA((max(len(pieces), 1),)),
            ],
        ),
        compiler_params=pltpu.CompilerParams(vmem_limit_bytes=26 * MIB),
        cost_estimate=pl.CostEstimate(
            flops=8 * terms * slots * blk**3, bytes_accessed=12 * right.size, transcendentals=0
        ),
    )(
        rows,
        limit,
        which,
        pltpu.with_memory_space_constraint(whole, pltpu.VMEM),
        *pieces, own, *near, *far, right, known, *states)


def finish_kernel(sums_ref, coef_ref, one_ref, other_ref, out_ref, energy_ref):
    sums = jnp.sum(sums_ref[...], axis=0)
    total = jnp.broadcast_to(jnp.sum(sums, axis=1, keepdims=True), sums.shape)
    lam, keep, turn = mix(coef_ref[4:5, :], total[0:1, :] + 1e-06, total[1:2, :])
    energy_ref[...] = jnp.broadcast_to(lam, energy_ref.shape)
    for slot in range(one_ref.shape[0]):
        out_ref[slot] = keep * one_ref[slot] + turn * other_ref[slot]


def finish(sums, coefs, one, other):
    return pl.pallas_call(
        finish_kernel,
        out_shape=[
            jax.ShapeDtypeStruct(one.shape, jnp.float32),
            jax.ShapeDtypeStruct(coefs.shape, jnp.float32),
        ],
        compiler_params=pltpu.CompilerParams(vmem_limit_bytes=4 * MIB),
    )(sums, coefs, one, other)


def partner(index, move):
    axis, flip = move
    z, y = index // SIDE, index % SIDE
    return z * SIDE + (y ^ flip) if axis == "y" else (z ^ flip) * SIDE + y


def swap(value, move, count):
    return lax.ppermute(value, "sector", [(index, partner(index, move)) for index in range(count)])


def lay_kernel(*refs):
    parts, (out_ref, sems) = refs[:-2], refs[-2:]
    copies = []
    at = 0
    for number, part in enumerate(parts):
        size = part.shape[0]
        copies.append(
            pltpu.make_async_copy(part, out_ref.at[pl.ds(at, size), :], sems.at[number])
        )
        at += size
    for copy in copies:
        copy.start()
    for copy in copies:
        copy.wait()


def lay(parts):
    total = sum(part.shape[0] for part in parts)
    return pl.pallas_call(
        lay_kernel,
        out_shape=pltpu.VMEM((total, parts[0].shape[1]), jnp.float32),
        in_specs=[pl.BlockSpec(memory_space=pl.ANY)] * len(parts),
        out_specs=pl.BlockSpec(memory_space=pltpu.VMEM),
        scratch_shapes=[pltpu.SemaphoreType.DMA((len(parts),))],
        compiler_params=pltpu.CompilerParams(vmem_limit_bytes=1 * MIB),
        cost_estimate=pl.CostEstimate(flops=0, bytes_accessed=8 * total * 128, transcendentals=0),
    )(*parts)


def gather(quarters, count):
    held = list(quarters)
    for step in range(len(ORDERS[0])):
        came = [swap(value, order[step], count) for value, order in zip(held, ORDERS)]
        if step == len(ORDERS[0]) - 1:
            return lay(held), came, held[0]
        held = [jnp.concatenate(pair, axis=0) for pair in zip(held, came)]


def place_of(apart, flips):
    first, second = flips
    both = first ^ second
    return jnp.where(apart == first, 1, jnp.where(apart == second, 2, jnp.where(apart == both, 3, 0)))


def block_rows(source, owner, sdev, blk):
    device, slot = source // sdev, source % sdev
    apart = device ^ owner
    apart = {"z": apart // SIDE, "y": apart % SIDE}
    per = sdev // PARTS
    sizes = heights(sdev, blk)
    units = SIDE * SIDE // 2
    rows = jnp.zeros_like(source)
    base = 0
    for part, order in enumerate(ORDERS):
        (near, one), (_, two), (far, three), (_, four) = order
        unit = place_of(apart[near], (one, two)) + SIDE * place_of(apart[far], (three, four))
        here = base + unit % units * sizes[part] + unit // units * units * sum(sizes)
        here = here + (slot % per) * blk
        rows = jnp.where(slot // per == part, here, rows)
        base += units * sizes[part]
    return rows


def to_next(value):
    count = lax.axis_size("chain")
    return lax.ppermute(value, "chain", [(source, source + 1) for source in range(count - 1)])


def to_next_round(value):
    count = lax.axis_size("chain")
    inside = [(source, source + 1) for source in range(0, count, 2)]
    places = [(source - 3) % count for source in range(1, count - 1, 2)]
    pairs = inside + list(zip(range(1, count - 1, 2), places))
    near = value = lax.ppermute(value, "chain", pairs)
    for _ in range(count // 2 - 2):
        pairs = [(place, (place - 2) % count) for place in places]
        value = lax.ppermute(value, "chain", pairs)
        places = [place for _, place in pairs]
    return near, value


def body(left_env, right_env, site_block, start_vec, slot_sector, couple, dims, kept):
    lenv = left_env[0]
    renv = right_env[0]
    site = site_block[0]
    start = start_vec[0]
    sdev = start.shape[0]
    blk = start.shape[1]
    nsec = slot_sector.shape[0]
    devices = nsec // sdev
    owner = lax.axis_index("sector")
    slots = owner * sdev + jnp.arange(sdev, dtype=jnp.int32)
    sector_ids = jnp.take(slot_sector, slots)
    inverse = jnp.zeros((nsec,), jnp.int32).at[slot_sector].set(jnp.arange(nsec, dtype=jnp.int32))
    source = inverse[couple[sector_ids]]
    rows = block_rows(source, owner, sdev, blk)

    chain = lax.axis_index("chain")
    which = jnp.where(chain == 0, 0, jnp.where(chain % 2 == 1, 1, 2)).astype(jnp.int32).reshape(1)
    terms = lenv.shape[0]

    def in_hbm(value):
        return pltpu.with_memory_space_constraint(value, pltpu.HBM)

    k0, limit, packed = begin(
        owner.astype(jnp.int32).reshape(1),
        *(in_hbm(value) for value in (slot_sector, dims, kept, start)),
    )
    site, k0 = lax.optimization_barrier((site, k0))
    lenv = in_hbm(lenv)
    whole = lax.all_gather(packed, "sector", axis=0, tiled=True)
    some = terms // 8
    sizes = [terms // 2, terms - terms // 2 - 2 * some, some, some]
    built = {}
    for number in (0, 2, 3, 1):
        part = update(lenv, site, sum(sizes[:number]), sizes[number])
        if number < 2:
            near = far = to_next(part)
        else:
            near, far = to_next_round(part)
        built[number] = tuple(in_hbm(value) for value in (part, near, far))
    parts, nears, fars = ([built[number][k] for number in range(len(sizes))] for k in range(3))
    lefts = lenv, nears, fars
    right = in_hbm(renv)

    height = sdev * blk + TAIL
    tails = [device * height + height - TAIL for device in range(devices)]
    first_rows = (source // sdev) * height + (source % sdev) * blk
    known = jnp.zeros((TAIL, blk), jnp.float32)
    known, y0, *quarters = apply(
        first_rows, limit, which, tails, whole, [], lefts, right, known, [k0]
    )
    sizes = heights(sdev, blk)
    units = SIDE * SIDE // 2
    tails = [
        half * units * sum(sizes) + unit * sizes[0] + sizes[0] - TAIL
        for half in range(2)
        for unit in range(units)
    ]
    held, came, first = gather(quarters, devices)
    updated = join(parts, first)
    held, came, updated = lax.optimization_barrier((held, came, updated))
    known, z1, *quarters = apply(
        rows, limit, which, tails, held, came, lefts, right, known, [k0, y0]
    )
    held, came, _ = gather(quarters, devices)
    known, x1, r2, sums = apply(
        rows, limit, which, tails, held, came, lefts, right, known, [k0, y0, z1]
    )
    for axis in ("y", "z"):
        others = [swap(sums, (axis, flip), devices) for flip in range(1, SIDE)]
        if axis == "y":
            sums = (sums + others[0]) + (others[1] + others[2])
    x2, energy = finish(jnp.stack([sums] + others), known, x1, r2)
    return (x2[None], updated[None], energy[0, :1])


def solution(mesh):
    placed = (
        P("chain", None, "sector", None, None),
        P("chain", None, "sector", None, None),
        P("chain", "sector", None, None),
        P("chain", "sector", None, None),
        P(),
        P(),
        P(),
        P(),
    )
    return jax.shard_map(
        body,
        mesh=mesh,
        in_specs=placed,
        out_specs=(
            P("chain", "sector", None, None),
            P("chain", None, "sector", None, None),
            P("chain"),
        ),
        check_vma=False,
    )
```

```python
import functools

import jax
import jax.numpy as jnp
from jax import lax
from jax.experimental import pallas as pl
from jax.experimental.pallas import tpu as pltpu
from jax.sharding import PartitionSpec as P

MIB = 1 << 20
TAIL = 8
PARTS = 4
SIDE = 4
PAIR = 2
AHEAD = 3
ORDERS = ((("y", 1), ("y", 3), ("z", 1), ("z", 3)), (("y", 3), ("y", 1), ("z", 3), ("z", 1)),
          (("z", 1), ("z", 3), ("y", 1), ("y", 3)), (("z", 3), ("z", 1), ("y", 3), ("y", 1)))


def split(value):
    high = value.astype(jnp.bfloat16)
    low = (value - high.astype(jnp.float32)).astype(jnp.bfloat16)
    return high, low


def dot(left, right):
    return jnp.dot(left, right, preferred_element_type=jnp.float32)


def right_factor(high, low):
    top = jnp.concatenate([high, low], axis=1)
    bottom = jnp.concatenate([high, jnp.zeros_like(low)], axis=1)
    return jnp.concatenate([top, bottom], axis=0)


def folded(value):
    half = value.shape[1] // 2
    return value[:, :half] + value[:, half:]


def update_kernel(left_ref, site_ref, out_ref, inner, outer):
    terms, slots, blk, _ = left_ref.shape

    @pl.when(pl.program_id(0) == 0)
    def _():
        for slot in range(slots):
            site = site_ref[slot]
            inner[slot] = right_factor(*split(site))
            high, low = split(site.T)
            outer[slot] = jnp.concatenate([high, low, high], axis=1)

    for slot in range(slots):
        first = [jnp.concatenate(split(left_ref[index, slot]), axis=1) for index in range(terms)]
        half = folded(dot(jnp.concatenate(first, axis=0), inner[slot]))
        high, low = split(half)
        columns = []
        for index in range(terms):
            rows = slice(index * blk, (index + 1) * blk)
            columns.append(jnp.concatenate([high[rows], high[rows], low[rows]], axis=0))
        both = dot(outer[slot], jnp.concatenate(columns, axis=1))
        for index in range(terms):
            value = both[:, index * blk : (index + 1) * blk]
            out_ref[index, slot] = value


def update(left, site, at, some):
    _, slots, blk, _ = left.shape
    pair = PAIR
    return pl.pallas_call(
        update_kernel,
        out_shape=jax.ShapeDtypeStruct((some, slots, blk, blk), jnp.float32),
        grid=(some // pair,),
        in_specs=[
            pl.BlockSpec((pair, slots, blk, blk), lambda t: (at // pair + t, 0, 0, 0)),
            pl.BlockSpec((slots, blk, blk), lambda t: (0, 0, 0)),
        ],
        out_specs=pl.BlockSpec((pair, slots, blk, blk), lambda t: (t, 0, 0, 0)),
        scratch_shapes=[
            pltpu.VMEM((slots, 2 * blk, 2 * blk), jnp.bfloat16),
            pltpu.VMEM((slots, blk, 3 * blk), jnp.bfloat16),
        ],
        compiler_params=pltpu.CompilerParams(vmem_limit_bytes=12 * MIB),
        cost_estimate=pl.CostEstimate(
            flops=8 * some * slots * blk**3,
            bytes_accessed=8 * some * slots * blk * blk,
            transcendentals=0,
        ),
    )(left, site)


def join_kernel(starts, *refs):
    parts, out_ref = refs[: len(starts) - 1], refs[-1]
    step = pl.program_id(0)
    for part, start, end in zip(parts, starts, starts[1:]):
        @pl.when((step >= start) & (step < end))
        def _(part=part):
            out_ref[...] = part[...]


def join(parts, after):
    shape = parts[0].shape[1:]
    starts = [0]
    for part in parts:
        starts.append(starts[-1] + part.shape[0] // PAIR)
    specs = [
        pl.BlockSpec(
            (PAIR,) + shape, lambda t, start=start, end=end: (jnp.clip(t - start, 0, end - start - 1), 0, 0, 0)
        )
        for start, end in zip(starts, starts[1:])
    ]
    return pl.pallas_call(
        functools.partial(join_kernel, starts),
        out_shape=jax.ShapeDtypeStruct((PAIR * starts[-1],) + shape, jnp.float32),
        grid=(starts[-1],),
        in_specs=specs + [pl.BlockSpec(memory_space=pl.ANY)],
        out_specs=pl.BlockSpec((PAIR,) + shape, lambda t: (t, 0, 0, 0)),
        compiler_params=pltpu.CompilerParams(vmem_limit_bytes=12 * MIB),
        cost_estimate=pl.CostEstimate(
            flops=0, bytes_accessed=8 * sum(part.size for part in parts), transcendentals=0
        ),
    )(*parts, after)


def masked(value, limit):
    rows = lax.broadcasted_iota(jnp.int32, value.shape, 0)
    columns = lax.broadcasted_iota(jnp.int32, value.shape, 1)
    return jnp.where(jnp.maximum(rows, columns) < limit, value, 0.0)


def put_quarter(slot, value, quarters):
    blk = value.shape[0]
    per = pl.num_programs(0) // PARTS
    at = pl.ds(pl.multiple_of((slot % per) * blk, blk), blk)
    for part, quarter in enumerate(quarters):
        @pl.when(slot // per == part)
        def _(quarter=quarter):
            quarter[at, :] = value


def tail_of(products):
    rows = [jnp.sum(product, axis=0, keepdims=True) for product in products]
    rows.append(jnp.zeros((TAIL - len(rows), rows[0].shape[1]), jnp.float32))
    return jnp.concatenate(rows, axis=0)


def put_sums(slot, products, tail):
    tail[...] = jnp.where(slot == 0, 0.0, tail[...]) + tail_of(products)


def begin_kernel(owner_ref, sector_ref, dims_ref, kept_ref, start_ref, full_ref, limit_ref, packed_ref):
    slots, blk, _ = start_ref.shape
    total = jnp.zeros((blk, blk), jnp.float32)
    for slot in range(slots):
        sector = sector_ref[owner_ref[0] * slots + slot]
        limit = dims_ref[sector] * kept_ref[sector]
        limit_ref[slot] = limit
        value = masked(start_ref[slot], limit)
        full_ref[slot] = value
        packed_ref[slot * blk : (slot + 1) * blk, :] = value
        total = total + value * value
    packed_ref[slots * blk :, :] = tail_of([total])


def heights(slots, blk):
    per = slots // PARTS * blk
    return [per + TAIL] + [per] * (PARTS - 1)


def whole_spec(shape):
    return pl.BlockSpec(shape, lambda s, *_: (0,) * len(shape))


def begin(owner, slot_sector, dims, kept, start):
    slots, blk, _ = start.shape
    vmem = pl.BlockSpec(memory_space=pltpu.VMEM)
    smem = pl.BlockSpec(memory_space=pltpu.SMEM)
    return pl.pallas_call(
        begin_kernel,
        out_shape=[
            jax.ShapeDtypeStruct(start.shape, jnp.float32),
            jax.ShapeDtypeStruct((slots,), jnp.int32),
        ]
        + [jax.ShapeDtypeStruct((slots * blk + TAIL, blk), jnp.float32)],
        in_specs=[smem] * 4 + [vmem],
        out_specs=[vmem, smem, vmem],
        compiler_params=pltpu.CompilerParams(vmem_limit_bytes=4 * MIB),
    )(owner, slot_sector, dims, kept, start)


def start_fetch(slot, which, lefts, right, left_copy, right_copy, sems):
    own, near, far = lefts
    pltpu.make_async_copy(right.at[:, slot], right_copy.at[:, slot], sems.at[0, slot]).start()
    for number in range(3):
        @pl.when(which == number)
        def _(number=number):
            at = 0
            for part, ref in enumerate((near, far)[number - 1] if number else near):
                here = slice(at, at + ref.shape[0])
                source = ref.at[:, slot] if number else own.at[here, slot]
                at += ref.shape[0]
                pltpu.make_async_copy(
                    source, left_copy.at[here, slot], sems.at[1 + part, slot]
                ).start()


def wait_fetch(slot, lefts, right, left_copy, right_copy, sems):
    pltpu.make_async_copy(right.at[:, slot], right_copy.at[:, slot], sems.at[0, slot]).wait()
    own, near, _ = lefts
    at = 0
    for part, ref in enumerate(near):
        here = slice(at, at + ref.shape[0])
        pltpu.make_async_copy(
            own.at[here, slot], left_copy.at[here, slot], sems.at[1 + part, slot]
        ).wait()
        at += ref.shape[0]


def mix(a, b2, rz):
    b = jnp.sqrt(b2)
    d = rz / b2
    lam = (a + d) / 2 - jnp.sqrt(((a - d) / 2) ** 2 + b2)
    q = lam - a
    n = jnp.sqrt(b2 + q * q)
    return lam, b / n, (q / b) / n


def next_coefs(mode, known, sums):
    row = lambda value, k: value[k : k + 1, :]
    total = jnp.broadcast_to(jnp.sum(sums, axis=1, keepdims=True), sums.shape)
    rows = [row(known, k) for k in range(5)]
    if mode == 1:
        rows[0] = 1.0 / jnp.sqrt(row(total, 0) + 1e-06)
    elif mode == 2:
        rows[1] = row(total, 0)
    else:
        xz, ry, rz, rr = (row(total, k) for k in range(4))
        a0 = rows[1]
        _, keep, turn = mix(a0, rr + 1e-06, rz)
        rows[2:4] = keep, turn
        rows[4] = keep * keep * a0 + keep * turn * (xz + ry) + turn * turn * rz
    rows.append(jnp.zeros((TAIL - len(rows), sums.shape[1]), jnp.float32))
    return jnp.concatenate(rows, axis=0)


def apply_kernel(mode, counts, tails, rows_ref, limit_ref, which_ref, *refs):
    refs = list(refs)
    whole, pieces, own, near, far = ([refs.pop(0) for _ in range(count)] for count in counts)
    whole = whole[0]
    split_row = whole.shape[0]
    lefts = own[0], near, far
    right, known_ref = refs.pop(0), refs.pop(0)
    states, outs = refs[:mode], refs[mode:-6]
    blocks, left_copy, right_copy, inner, sems, piece_sems = refs[-6:]
    terms, _, blk, _ = left_copy.shape
    slot = pl.program_id(0)
    coef_ref = outs[0]
    outs = outs[1:]

    def rows_of(row, number):
        if not pieces:
            return whole[pl.ds(row, number), :]
        early = whole[pl.ds(pl.multiple_of(jnp.minimum(row, split_row - number), 8), number), :]
        late = blocks[pl.ds(pl.multiple_of(jnp.maximum(row - split_row, 0), 8), number), :]
        return jnp.where(row < split_row, early, late)

    @pl.when(slot == 0)
    def _():
        copies = []
        at = 0
        for number, piece in enumerate(pieces):
            size = piece.shape[0]
            copies.append(
                pltpu.make_async_copy(piece, blocks.at[pl.ds(at, size), :], piece_sems.at[number])
            )
            at += size
        for copy in copies:
            copy.start()
        for early in range(AHEAD):
            start_fetch(early, which_ref[0], lefts, right, left_copy, right_copy, sems)
        for copy in copies:
            copy.wait()
        sums = None
        for tail in tails:
            source, at = (whole, tail) if tail < split_row else (blocks, tail - split_row)
            part = source[at : at + TAIL, :]
            sums = part if sums is None else sums + part
        coef_ref[...] = next_coefs(mode, known_ref[...], sums)

    @pl.when(slot + AHEAD < pl.num_programs(0))
    def _():
        start_fetch(slot + AHEAD, which_ref[0], lefts, right, left_copy, right_copy, sems)

    wait_fetch(slot, lefts, right, left_copy, right_copy, sems)
    for term in range(terms):
        row = pl.multiple_of(rows_ref[slot, term], 8)
        first = jnp.concatenate(split(rows_of(row, blk)), axis=1)
        value = folded(dot(first, right_factor(*split(right_copy[term, slot]))))
        inner[term * blk : (term + 1) * blk, :] = jnp.concatenate(split(value), axis=1)
    result = None
    for term in range(0, terms, 2):
        (high0, low0), (high1, low1) = (
            split(left_copy[index, slot]) for index in (term, term + 1)
        )
        below = inner[term * blk : (term + 2) * blk, :]
        part = folded(dot(jnp.concatenate([high0, high1], axis=1), below))
        part = part + dot(jnp.concatenate([low0, low1], axis=1), below[:, :blk])
        result = part if result is None else result + part
    value = masked(result, limit_ref[slot])

    scale, a0, keep, turn, a1 = (coef_ref[k : k + 1, :] for k in range(5))
    x0 = states[0][0] * scale
    if mode == 1:
        y0 = value * scale
        products = [x0 * y0]
        send = y0
    else:
        y0 = states[1][0]
        r1 = y0 - a0 * x0
        if mode == 2:
            z1 = value - a0 * y0
            products = [x0 * z1, r1 * y0, r1 * z1, r1 * r1]
            send = z1
        else:
            z1 = states[2][0]
            x1 = keep * x0 + turn * r1
            y1 = keep * y0 + turn * z1
            r2 = y1 - a1 * x1
            z2 = keep * (z1 + a0 * y0) + turn * value - a1 * y1
            outs[0][0] = x1
            outs[1][0] = r2
            put_sums(slot, [r2 * r2, r2 * z2], outs[2])
            return
    outs[0][0] = send
    put_quarter(slot, send, outs[1:])
    put_sums(slot, products, outs[1].at[pl.ds(outs[1].shape[0] - TAIL, TAIL), :])


def apply(rows, limit, which, tails, whole, pieces, lefts, right, known, states):
    mode = len(states)
    terms, slots, blk, _ = right.shape
    vector = jax.ShapeDtypeStruct((slots, blk, blk), jnp.float32)
    vector_spec = pl.BlockSpec((1, blk, blk), lambda s, *_: (s, 0, 0))
    few = jax.ShapeDtypeStruct((TAIL, blk), jnp.float32)
    few_spec = whole_spec((TAIL, blk))
    if mode < 3:
        sizes = heights(slots, blk)
        out_shape = [few, vector]
        out_shape += [jax.ShapeDtypeStruct((size, blk), jnp.float32) for size in sizes]
        out_specs = [few_spec, vector_spec] + [whole_spec((size, blk)) for size in sizes]
    else:
        out_shape = [few, vector, vector, few]
        out_specs = [few_spec, vector_spec, vector_spec, few_spec]
    total = sum(piece.shape[0] for piece in pieces) or TAIL
    own, near, far = lefts
    counts = (1, len(pieces), 1, len(near), len(far))
    return pl.pallas_call(
        functools.partial(apply_kernel, mode, counts, tails),
        out_shape=out_shape,
        grid_spec=pltpu.PrefetchScalarGridSpec(
            num_scalar_prefetch=3,
            grid=(slots,),
            in_specs=[pl.BlockSpec(memory_space=pltpu.VMEM)]
            + [pl.BlockSpec(memory_space=pl.ANY)] * sum(counts)
            + [few_spec]
            + [vector_spec] * mode,
            out_specs=out_specs,
            scratch_shapes=[
                pltpu.VMEM((total, blk), jnp.float32),
                pltpu.VMEM(right.shape, jnp.float32),
                pltpu.VMEM(right.shape, jnp.float32),
                pltpu.VMEM((terms * blk, 2 * blk), jnp.bfloat16),
                pltpu.SemaphoreType.DMA((1 + len(near), slots)),
                pltpu.SemaphoreType.DMA((max(len(pieces), 1),)),
            ],
        ),
        compiler_params=pltpu.CompilerParams(vmem_limit_bytes=26 * MIB),
        cost_estimate=pl.CostEstimate(
            flops=8 * terms * slots * blk**3, bytes_accessed=12 * right.size, transcendentals=0
        ),
    )(
        rows,
        limit,
        which,
        pltpu.with_memory_space_constraint(whole, pltpu.VMEM),
        *pieces, own, *near, *far, right, known, *states)


def finish_kernel(sums_ref, coef_ref, one_ref, other_ref, out_ref, energy_ref):
    sums = jnp.sum(sums_ref[...], axis=0)
    total = jnp.broadcast_to(jnp.sum(sums, axis=1, keepdims=True), sums.shape)
    lam, keep, turn = mix(coef_ref[4:5, :], total[0:1, :] + 1e-06, total[1:2, :])
    energy_ref[...] = jnp.broadcast_to(lam, energy_ref.shape)
    for slot in range(one_ref.shape[0]):
        out_ref[slot] = keep * one_ref[slot] + turn * other_ref[slot]


def finish(sums, coefs, one, other):
    return pl.pallas_call(
        finish_kernel,
        out_shape=[
            jax.ShapeDtypeStruct(one.shape, jnp.float32),
            jax.ShapeDtypeStruct(coefs.shape, jnp.float32),
        ],
        compiler_params=pltpu.CompilerParams(vmem_limit_bytes=4 * MIB),
    )(sums, coefs, one, other)


def partner(index, move):
    axis, flip = move
    z, y = index // SIDE, index % SIDE
    return z * SIDE + (y ^ flip) if axis == "y" else (z ^ flip) * SIDE + y


def swap(value, move, count):
    return lax.ppermute(value, "sector", [(index, partner(index, move)) for index in range(count)])


def lay_kernel(*refs):
    parts, (out_ref, sems) = refs[:-2], refs[-2:]
    copies = []
    at = 0
    for number, part in enumerate(parts):
        size = part.shape[0]
        copies.append(
            pltpu.make_async_copy(part, out_ref.at[pl.ds(at, size), :], sems.at[number])
        )
        at += size
    for copy in copies:
        copy.start()
    for copy in copies:
        copy.wait()


def lay(parts):
    total = sum(part.shape[0] for part in parts)
    return pl.pallas_call(
        lay_kernel,
        out_shape=pltpu.VMEM((total, parts[0].shape[1]), jnp.float32),
        in_specs=[pl.BlockSpec(memory_space=pl.ANY)] * len(parts),
        out_specs=pl.BlockSpec(memory_space=pltpu.VMEM),
        scratch_shapes=[pltpu.SemaphoreType.DMA((len(parts),))],
        compiler_params=pltpu.CompilerParams(vmem_limit_bytes=1 * MIB),
        cost_estimate=pl.CostEstimate(flops=0, bytes_accessed=8 * total * 128, transcendentals=0),
    )(*parts)


def gather(quarters, count):
    held = list(quarters)
    for step in range(len(ORDERS[0])):
        came = [swap(value, order[step], count) for value, order in zip(held, ORDERS)]
        if step == len(ORDERS[0]) - 1:
            return lay(held), came, held[0]
        held = [jnp.concatenate(pair, axis=0) for pair in zip(held, came)]


def place_of(apart, flips):
    first, second = flips
    both = first ^ second
    return jnp.where(apart == first, 1, jnp.where(apart == second, 2, jnp.where(apart == both, 3, 0)))


def block_rows(source, owner, sdev, blk):
    device, slot = source // sdev, source % sdev
    apart = device ^ owner
    apart = {"z": apart // SIDE, "y": apart % SIDE}
    per = sdev // PARTS
    sizes = heights(sdev, blk)
    units = SIDE * SIDE // 2
    rows = jnp.zeros_like(source)
    base = 0
    for part, order in enumerate(ORDERS):
        (near, one), (_, two), (far, three), (_, four) = order
        unit = place_of(apart[near], (one, two)) + SIDE * place_of(apart[far], (three, four))
        here = base + unit % units * sizes[part] + unit // units * units * sum(sizes)
        here = here + (slot % per) * blk
        rows = jnp.where(slot // per == part, here, rows)
        base += units * sizes[part]
    return rows


def to_next(value):
    count = lax.axis_size("chain")
    return lax.ppermute(value, "chain", [(source, source + 1) for source in range(count - 1)])


def to_next_round(value):
    count = lax.axis_size("chain")
    inside = [(source, source + 1) for source in range(0, count, 2)]
    places = [(source - 3) % count for source in range(1, count - 1, 2)]
    pairs = inside + list(zip(range(1, count - 1, 2), places))
    near = value = lax.ppermute(value, "chain", pairs)
    for _ in range(count // 2 - 2):
        pairs = [(place, (place - 2) % count) for place in places]
        value = lax.ppermute(value, "chain", pairs)
        places = [place for _, place in pairs]
    return near, value


def body(left_env, right_env, site_block, start_vec, slot_sector, couple, dims, kept):
    lenv = left_env[0]
    renv = right_env[0]
    site = site_block[0]
    start = start_vec[0]
    sdev = start.shape[0]
    blk = start.shape[1]
    nsec = slot_sector.shape[0]
    devices = nsec // sdev
    owner = lax.axis_index("sector")
    slots = owner * sdev + jnp.arange(sdev, dtype=jnp.int32)
    sector_ids = jnp.take(slot_sector, slots)
    inverse = jnp.zeros((nsec,), jnp.int32).at[slot_sector].set(jnp.arange(nsec, dtype=jnp.int32))
    source = inverse[couple[sector_ids]]
    rows = block_rows(source, owner, sdev, blk)

    chain = lax.axis_index("chain")
    which = jnp.where(chain == 0, 0, jnp.where(chain % 2 == 1, 1, 2)).astype(jnp.int32).reshape(1)
    terms = lenv.shape[0]

    def in_hbm(value):
        return pltpu.with_memory_space_constraint(value, pltpu.HBM)

    k0, limit, packed = begin(
        owner.astype(jnp.int32).reshape(1),
        *(in_hbm(value) for value in (slot_sector, dims, kept, start)),
    )
    site, k0 = lax.optimization_barrier((site, k0))
    lenv = in_hbm(lenv)
    whole = lax.all_gather(packed, "sector", axis=0, tiled=True)
    some = terms // 8
    sizes = [terms // 2, terms - terms // 2 - 2 * some, some, some]
    built = {}
    for number in (0, 2, 3, 1):
        part = update(lenv, site, sum(sizes[:number]), sizes[number])
        if number < 2:
            near = far = to_next(part)
        else:
            near, far = to_next_round(part)
        built[number] = tuple(in_hbm(value) for value in (part, near, far))
    parts, nears, fars = ([built[number][k] for number in range(len(sizes))] for k in range(3))
    lefts = lenv, nears, fars
    right = in_hbm(renv)

    height = sdev * blk + TAIL
    tails = [device * height + height - TAIL for device in range(devices)]
    first_rows = (source // sdev) * height + (source % sdev) * blk
    known = jnp.zeros((TAIL, blk), jnp.float32)
    known, y0, *quarters = apply(
        first_rows, limit, which, tails, lay([in_hbm(whole)]), [], lefts, right, known, [k0]
    )
    sizes = heights(sdev, blk)
    units = SIDE * SIDE // 2
    tails = [
        half * units * sum(sizes) + unit * sizes[0] + sizes[0] - TAIL
        for half in range(2)
        for unit in range(units)
    ]
    held, came, first = gather(quarters, devices)
    updated = join(parts, first)
    held, came, updated = lax.optimization_barrier((held, came, updated))
    known, z1, *quarters = apply(
        rows, limit, which, tails, held, came, lefts, right, known, [k0, y0]
    )
    held, came, _ = gather(quarters, devices)
    known, x1, r2, sums = apply(
        rows, limit, which, tails, held, came, lefts, right, known, [k0, y0, z1]
    )
    for axis in ("y", "z"):
        others = [swap(sums, (axis, flip), devices) for flip in range(1, SIDE)]
        if axis == "y":
            sums = (sums + others[0]) + (others[1] + others[2])
    x2, energy = finish(jnp.stack([sums] + others), known, x1, r2)
    return (x2[None], updated[None], energy[0, :1])


def solution(mesh):
    placed = (
        P("chain", None, "sector", None, None),
        P("chain", None, "sector", None, None),
        P("chain", "sector", None, None),
        P("chain", "sector", None, None),
        P(),
        P(),
        P(),
        P(),
    )
    return jax.shard_map(
        body,
        mesh=mesh,
        in_specs=placed,
        out_specs=(
            P("chain", "sector", None, None),
            P("chain", None, "sector", None, None),
            P("chain"),
        ),
        check_vma=False,
    )
```

```python
import functools

import jax
import jax.numpy as jnp
from jax import lax
from jax.experimental import pallas as pl
from jax.experimental.pallas import tpu as pltpu
from jax.sharding import PartitionSpec as P

MIB = 1 << 20
TAIL = 8
PARTS = 4
SIDE = 4
PAIR = 2
AHEAD = 4
TOGETHER = 2
ORDERS = ((("y", 1), ("y", 3), ("z", 1), ("z", 3)), (("y", 3), ("y", 1), ("z", 3), ("z", 1)),
          (("z", 1), ("z", 3), ("y", 1), ("y", 3)), (("z", 3), ("z", 1), ("y", 3), ("y", 1)))


def split(value):
    high = value.astype(jnp.bfloat16)
    low = (value - high.astype(jnp.float32)).astype(jnp.bfloat16)
    return high, low


def dot(left, right):
    return jnp.dot(left, right, preferred_element_type=jnp.float32)


def right_factor(high, low):
    top = jnp.concatenate([high, low], axis=1)
    bottom = jnp.concatenate([high, jnp.zeros_like(low)], axis=1)
    return jnp.concatenate([top, bottom], axis=0)


def folded(value):
    half = value.shape[1] // 2
    return value[:, :half] + value[:, half:]


def update_kernel(left_ref, site_ref, out_ref, inner, outer):
    terms, slots, blk, _ = left_ref.shape

    @pl.when(pl.program_id(0) == 0)
    def _():
        for slot in range(slots):
            site = site_ref[slot]
            inner[slot] = right_factor(*split(site))
            high, low = split(site.T)
            outer[slot] = jnp.concatenate([high, low, high], axis=1)

    for slot in range(slots):
        first = [jnp.concatenate(split(left_ref[index, slot]), axis=1) for index in range(terms)]
        half = folded(dot(jnp.concatenate(first, axis=0), inner[slot]))
        high, low = split(half)
        columns = []
        for index in range(terms):
            rows = slice(index * blk, (index + 1) * blk)
            columns.append(jnp.concatenate([high[rows], high[rows], low[rows]], axis=0))
        both = dot(outer[slot], jnp.concatenate(columns, axis=1))
        for index in range(terms):
            value = both[:, index * blk : (index + 1) * blk]
            out_ref[index, slot] = value


def update(left, site, at, some):
    _, slots, blk, _ = left.shape
    pair = PAIR
    return pl.pallas_call(
        update_kernel,
        out_shape=jax.ShapeDtypeStruct((some, slots, blk, blk), jnp.float32),
        grid=(some // pair,),
        in_specs=[
            pl.BlockSpec((pair, slots, blk, blk), lambda t: (at // pair + t, 0, 0, 0)),
            pl.BlockSpec((slots, blk, blk), lambda t: (0, 0, 0)),
        ],
        out_specs=pl.BlockSpec((pair, slots, blk, blk), lambda t: (t, 0, 0, 0)),
        scratch_shapes=[
            pltpu.VMEM((slots, 2 * blk, 2 * blk), jnp.bfloat16),
            pltpu.VMEM((slots, blk, 3 * blk), jnp.bfloat16),
        ],
        compiler_params=pltpu.CompilerParams(vmem_limit_bytes=12 * MIB),
        cost_estimate=pl.CostEstimate(
            flops=8 * some * slots * blk**3,
            bytes_accessed=8 * some * slots * blk * blk,
            transcendentals=0,
        ),
    )(left, site)


def join_kernel(starts, *refs):
    parts, out_ref = refs[: len(starts) - 1], refs[-1]
    step = pl.program_id(0)
    for part, start, end in zip(parts, starts, starts[1:]):
        @pl.when((step >= start) & (step < end))
        def _(part=part):
            out_ref[...] = part[...]


def join(parts, after):
    shape = parts[0].shape[1:]
    starts = [0]
    for part in parts:
        starts.append(starts[-1] + part.shape[0] // PAIR)
    specs = [
        pl.BlockSpec(
            (PAIR,) + shape, lambda t, start=start, end=end: (jnp.clip(t - start, 0, end - start - 1), 0, 0, 0)
        )
        for start, end in zip(starts, starts[1:])
    ]
    return pl.pallas_call(
        functools.partial(join_kernel, starts),
        out_shape=jax.ShapeDtypeStruct((PAIR * starts[-1],) + shape, jnp.float32),
        grid=(starts[-1],),
        in_specs=specs + [pl.BlockSpec(memory_space=pl.ANY)],
        out_specs=pl.BlockSpec((PAIR,) + shape, lambda t: (t, 0, 0, 0)),
        compiler_params=pltpu.CompilerParams(vmem_limit_bytes=12 * MIB),
        cost_estimate=pl.CostEstimate(
            flops=0, bytes_accessed=8 * sum(part.size for part in parts), transcendentals=0
        ),
    )(*parts, after)


def masked(value, limit):
    rows = lax.broadcasted_iota(jnp.int32, value.shape, 0)
    columns = lax.broadcasted_iota(jnp.int32, value.shape, 1)
    return jnp.where(jnp.maximum(rows, columns) < limit, value, 0.0)


def put_quarter(slot, value, quarters):
    blk = value.shape[0]
    per = pl.num_programs(0) * TOGETHER // PARTS
    at = pl.ds(pl.multiple_of((slot % per) * blk, blk), blk)
    for part, quarter in enumerate(quarters):
        @pl.when(slot // per == part)
        def _(quarter=quarter):
            quarter[at, :] = value


def tail_of(products):
    rows = [jnp.sum(product, axis=0, keepdims=True) for product in products]
    rows.append(jnp.zeros((TAIL - len(rows), rows[0].shape[1]), jnp.float32))
    return jnp.concatenate(rows, axis=0)


def put_sums(slot, products, tail):
    tail[...] = jnp.where(slot == 0, 0.0, tail[...]) + tail_of(products)


def begin_kernel(owner_ref, sector_ref, dims_ref, kept_ref, start_ref, full_ref, limit_ref, packed_ref):
    slots, blk, _ = start_ref.shape
    total = jnp.zeros((blk, blk), jnp.float32)
    for slot in range(slots):
        sector = sector_ref[owner_ref[0] * slots + slot]
        limit = dims_ref[sector] * kept_ref[sector]
        limit_ref[slot] = limit
        value = masked(start_ref[slot], limit)
        full_ref[slot] = value
        packed_ref[slot * blk : (slot + 1) * blk, :] = value
        total = total + value * value
    packed_ref[slots * blk :, :] = tail_of([total])


def heights(slots, blk):
    per = slots // PARTS * blk
    return [per + TAIL] + [per] * (PARTS - 1)


def whole_spec(shape):
    return pl.BlockSpec(shape, lambda s, *_: (0,) * len(shape))


def begin(owner, slot_sector, dims, kept, start):
    slots, blk, _ = start.shape
    vmem = pl.BlockSpec(memory_space=pltpu.VMEM)
    smem = pl.BlockSpec(memory_space=pltpu.SMEM)
    return pl.pallas_call(
        begin_kernel,
        out_shape=[
            jax.ShapeDtypeStruct(start.shape, jnp.float32),
            jax.ShapeDtypeStruct((slots,), jnp.int32),
        ]
        + [jax.ShapeDtypeStruct((slots * blk + TAIL, blk), jnp.float32)],
        in_specs=[smem] * 4 + [vmem],
        out_specs=[vmem, smem, vmem],
        compiler_params=pltpu.CompilerParams(vmem_limit_bytes=4 * MIB),
    )(owner, slot_sector, dims, kept, start)


def start_fetch(slot, which, lefts, right, left_copy, right_copy, sems):
    own, near, far = lefts
    pltpu.make_async_copy(right.at[:, slot], right_copy.at[:, slot], sems.at[0, slot]).start()
    for number in range(3):
        @pl.when(which == number)
        def _(number=number):
            at = 0
            for part, ref in enumerate((near, far)[number - 1] if number else near):
                here = slice(at, at + ref.shape[0])
                source = ref.at[:, slot] if number else own.at[here, slot]
                at += ref.shape[0]
                pltpu.make_async_copy(
                    source, left_copy.at[here, slot], sems.at[1 + part, slot]
                ).start()


def wait_fetch(slot, lefts, right, left_copy, right_copy, sems):
    pltpu.make_async_copy(right.at[:, slot], right_copy.at[:, slot], sems.at[0, slot]).wait()
    own, near, _ = lefts
    at = 0
    for part, ref in enumerate(near):
        here = slice(at, at + ref.shape[0])
        pltpu.make_async_copy(
            own.at[here, slot], left_copy.at[here, slot], sems.at[1 + part, slot]
        ).wait()
        at += ref.shape[0]


def mix(a, b2, rz):
    b = jnp.sqrt(b2)
    d = rz / b2
    lam = (a + d) / 2 - jnp.sqrt(((a - d) / 2) ** 2 + b2)
    q = lam - a
    n = jnp.sqrt(b2 + q * q)
    return lam, b / n, (q / b) / n


def next_coefs(mode, known, sums):
    row = lambda value, k: value[k : k + 1, :]
    total = jnp.broadcast_to(jnp.sum(sums, axis=1, keepdims=True), sums.shape)
    rows = [row(known, k) for k in range(5)]
    if mode == 1:
        rows[0] = 1.0 / jnp.sqrt(row(total, 0) + 1e-06)
    elif mode == 2:
        rows[1] = row(total, 0)
    else:
        xz, ry, rz, rr = (row(total, k) for k in range(4))
        a0 = rows[1]
        _, keep, turn = mix(a0, rr + 1e-06, rz)
        rows[2:4] = keep, turn
        rows[4] = keep * keep * a0 + keep * turn * (xz + ry) + turn * turn * rz
    rows.append(jnp.zeros((TAIL - len(rows), sums.shape[1]), jnp.float32))
    return jnp.concatenate(rows, axis=0)


def apply_kernel(mode, counts, tails, rows_ref, limit_ref, which_ref, *refs):
    refs = list(refs)
    whole, pieces, own, near, far = ([refs.pop(0) for _ in range(count)] for count in counts)
    whole = whole[0]
    split_row = whole.shape[0]
    lefts = own[0], near, far
    right, known_ref = refs.pop(0), refs.pop(0)
    states, outs = refs[:mode], refs[mode:-6]
    blocks, left_copy, right_copy, inner, sems, piece_sems = refs[-6:]
    terms, slots, blk, _ = left_copy.shape
    step = pl.program_id(0)
    coef_ref = outs[0]
    outs = outs[1:]

    def rows_of(row, number):
        if not pieces:
            return whole[pl.ds(row, number), :]
        early = whole[pl.ds(pl.multiple_of(jnp.minimum(row, split_row - number), 8), number), :]
        late = blocks[pl.ds(pl.multiple_of(jnp.maximum(row - split_row, 0), 8), number), :]
        return jnp.where(row < split_row, early, late)

    @pl.when(step == 0)
    def _():
        copies = []
        at = 0
        for number, piece in enumerate(pieces):
            size = piece.shape[0]
            copies.append(
                pltpu.make_async_copy(piece, blocks.at[pl.ds(at, size), :], piece_sems.at[number])
            )
            at += size
        for copy in copies:
            copy.start()
        for early in range(AHEAD):
            start_fetch(early, which_ref[0], lefts, right, left_copy, right_copy, sems)
        for copy in copies:
            copy.wait()
        sums = None
        for tail in tails:
            source, at = (whole, tail) if tail < split_row else (blocks, tail - split_row)
            part = source[at : at + TAIL, :]
            sums = part if sums is None else sums + part
        coef_ref[...] = next_coefs(mode, known_ref[...], sums)

    def product(slot, inner):
        for term in range(terms):
            row = pl.multiple_of(rows_ref[slot, term], 8)
            first = jnp.concatenate(split(rows_of(row, blk)), axis=1)
            value = folded(dot(first, right_factor(*split(right_copy[term, slot]))))
            inner[term * blk : (term + 1) * blk, :] = jnp.concatenate(split(value), axis=1)
        result = None
        for term in range(0, terms, 2):
            (high0, low0), (high1, low1) = (
                split(left_copy[index, slot]) for index in (term, term + 1)
            )
            below = inner[term * blk : (term + 2) * blk, :]
            part = folded(dot(jnp.concatenate([high0, high1], axis=1), below))
            part = part + dot(jnp.concatenate([low0, low1], axis=1), below[:, :blk])
            result = part if result is None else result + part
        return masked(result, limit_ref[slot])

    first_slot = step * TOGETHER

    @pl.when(first_slot + AHEAD < slots)
    def _():
        for more in range(TOGETHER):
            start_fetch(
                first_slot + AHEAD + more, which_ref[0], lefts, right, left_copy, right_copy, sems
            )

    for more in range(TOGETHER):
        wait_fetch(first_slot + more, lefts, right, left_copy, right_copy, sems)
    values = []
    for more in range(TOGETHER):
        values.append(product(first_slot + more, inner.at[more]))
    scale, a0, keep, turn, a1 = (coef_ref[k : k + 1, :] for k in range(5))
    for more, value in enumerate(values):
        slot = first_slot + more

        x0 = states[0][more] * scale
        if mode == 1:
            y0 = value * scale
            products = [x0 * y0]
            send = y0
        else:
            y0 = states[1][more]
            r1 = y0 - a0 * x0
            if mode == 2:
                z1 = value - a0 * y0
                products = [x0 * z1, r1 * y0, r1 * z1, r1 * r1]
                send = z1
            else:
                z1 = states[2][more]
                x1 = keep * x0 + turn * r1
                y1 = keep * y0 + turn * z1
                r2 = y1 - a1 * x1
                z2 = keep * (z1 + a0 * y0) + turn * value - a1 * y1
                outs[0][more] = x1
                outs[1][more] = r2
                put_sums(slot, [r2 * r2, r2 * z2], outs[2])
                continue
        outs[0][more] = send
        put_quarter(slot, send, outs[1:])
        put_sums(slot, products, outs[1].at[pl.ds(outs[1].shape[0] - TAIL, TAIL), :])


def apply(rows, limit, which, tails, whole, pieces, lefts, right, known, states):
    mode = len(states)
    terms, slots, blk, _ = right.shape
    vector = jax.ShapeDtypeStruct((slots, blk, blk), jnp.float32)
    vector_spec = pl.BlockSpec((TOGETHER, blk, blk), lambda s, *_: (s, 0, 0))
    few = jax.ShapeDtypeStruct((TAIL, blk), jnp.float32)
    few_spec = whole_spec((TAIL, blk))
    if mode < 3:
        sizes = heights(slots, blk)
        out_shape = [few, vector]
        out_shape += [jax.ShapeDtypeStruct((size, blk), jnp.float32) for size in sizes]
        out_specs = [few_spec, vector_spec] + [whole_spec((size, blk)) for size in sizes]
    else:
        out_shape = [few, vector, vector, few]
        out_specs = [few_spec, vector_spec, vector_spec, few_spec]
    total = sum(piece.shape[0] for piece in pieces) or TAIL
    own, near, far = lefts
    counts = (1, len(pieces), 1, len(near), len(far))
    return pl.pallas_call(
        functools.partial(apply_kernel, mode, counts, tails),
        out_shape=out_shape,
        grid_spec=pltpu.PrefetchScalarGridSpec(
            num_scalar_prefetch=3,
            grid=(slots // TOGETHER,),
            in_specs=[pl.BlockSpec(memory_space=pltpu.VMEM)]
            + [pl.BlockSpec(memory_space=pl.ANY)] * sum(counts)
            + [few_spec]
            + [vector_spec] * mode,
            out_specs=out_specs,
            scratch_shapes=[
                pltpu.VMEM((total, blk), jnp.float32),
                pltpu.VMEM(right.shape, jnp.float32),
                pltpu.VMEM(right.shape, jnp.float32),
                pltpu.VMEM((TOGETHER, terms * blk, 2 * blk), jnp.bfloat16),
                pltpu.SemaphoreType.DMA((1 + len(near), slots)),
                pltpu.SemaphoreType.DMA((max(len(pieces), 1),)),
            ],
        ),
        compiler_params=pltpu.CompilerParams(vmem_limit_bytes=28 * MIB),
        cost_estimate=pl.CostEstimate(
            flops=8 * terms * slots * blk**3, bytes_accessed=12 * right.size, transcendentals=0
        ),
    )(
        rows,
        limit,
        which,
        pltpu.with_memory_space_constraint(whole, pltpu.VMEM),
        *pieces, own, *near, *far, right, known, *states)


def finish_kernel(sums_ref, coef_ref, one_ref, other_ref, out_ref, energy_ref):
    sums = jnp.sum(sums_ref[...], axis=0)
    total = jnp.broadcast_to(jnp.sum(sums, axis=1, keepdims=True), sums.shape)
    lam, keep, turn = mix(coef_ref[4:5, :], total[0:1, :] + 1e-06, total[1:2, :])
    energy_ref[...] = jnp.broadcast_to(lam, energy_ref.shape)
    for slot in range(one_ref.shape[0]):
        out_ref[slot] = keep * one_ref[slot] + turn * other_ref[slot]


def finish(sums, coefs, one, other):
    return pl.pallas_call(
        finish_kernel,
        out_shape=[
            jax.ShapeDtypeStruct(one.shape, jnp.float32),
            jax.ShapeDtypeStruct(coefs.shape, jnp.float32),
        ],
        compiler_params=pltpu.CompilerParams(vmem_limit_bytes=4 * MIB),
    )(sums, coefs, one, other)


def partner(index, move):
    axis, flip = move
    z, y = index // SIDE, index % SIDE
    return z * SIDE + (y ^ flip) if axis == "y" else (z ^ flip) * SIDE + y


def swap(value, move, count):
    return lax.ppermute(value, "sector", [(index, partner(index, move)) for index in range(count)])


def lay_kernel(*refs):
    parts, (out_ref, sems) = refs[:-2], refs[-2:]
    copies = []
    at = 0
    for number, part in enumerate(parts):
        size = part.shape[0]
        copies.append(
            pltpu.make_async_copy(part, out_ref.at[pl.ds(at, size), :], sems.at[number])
        )
        at += size
    for copy in copies:
        copy.start()
    for copy in copies:
        copy.wait()


def lay(parts):
    total = sum(part.shape[0] for part in parts)
    return pl.pallas_call(
        lay_kernel,
        out_shape=pltpu.VMEM((total, parts[0].shape[1]), jnp.float32),
        in_specs=[pl.BlockSpec(memory_space=pl.ANY)] * len(parts),
        out_specs=pl.BlockSpec(memory_space=pltpu.VMEM),
        scratch_shapes=[pltpu.SemaphoreType.DMA((len(parts),))],
        compiler_params=pltpu.CompilerParams(vmem_limit_bytes=1 * MIB),
        cost_estimate=pl.CostEstimate(flops=0, bytes_accessed=8 * total * 128, transcendentals=0),
    )(*parts)


def gather(quarters, count):
    held = list(quarters)
    for step in range(len(ORDERS[0])):
        came = [swap(value, order[step], count) for value, order in zip(held, ORDERS)]
        if step == len(ORDERS[0]) - 1:
            return lay(held), came, held[0]
        held = [jnp.concatenate(pair, axis=0) for pair in zip(held, came)]


def place_of(apart, flips):
    first, second = flips
    both = first ^ second
    return jnp.where(apart == first, 1, jnp.where(apart == second, 2, jnp.where(apart == both, 3, 0)))


def block_rows(source, owner, sdev, blk):
    device, slot = source // sdev, source % sdev
    apart = device ^ owner
    apart = {"z": apart // SIDE, "y": apart % SIDE}
    per = sdev // PARTS
    sizes = heights(sdev, blk)
    units = SIDE * SIDE // 2
    rows = jnp.zeros_like(source)
    base = 0
    for part, order in enumerate(ORDERS):
        (near, one), (_, two), (far, three), (_, four) = order
        unit = place_of(apart[near], (one, two)) + SIDE * place_of(apart[far], (three, four))
        here = base + unit % units * sizes[part] + unit // units * units * sum(sizes)
        here = here + (slot % per) * blk
        rows = jnp.where(slot // per == part, here, rows)
        base += units * sizes[part]
    return rows


def to_next(value):
    count = lax.axis_size("chain")
    return lax.ppermute(value, "chain", [(source, source + 1) for source in range(count - 1)])


def to_next_round(value):
    count = lax.axis_size("chain")
    inside = [(source, source + 1) for source in range(0, count, 2)]
    places = [(source - 3) % count for source in range(1, count - 1, 2)]
    pairs = inside + list(zip(range(1, count - 1, 2), places))
    near = value = lax.ppermute(value, "chain", pairs)
    for _ in range(count // 2 - 2):
        pairs = [(place, (place - 2) % count) for place in places]
        value = lax.ppermute(value, "chain", pairs)
        places = [place for _, place in pairs]
    return near, value


def body(left_env, right_env, site_block, start_vec, slot_sector, couple, dims, kept):
    lenv = left_env[0]
    renv = right_env[0]
    site = site_block[0]
    start = start_vec[0]
    sdev = start.shape[0]
    blk = start.shape[1]
    nsec = slot_sector.shape[0]
    devices = nsec // sdev
    owner = lax.axis_index("sector")
    slots = owner * sdev + jnp.arange(sdev, dtype=jnp.int32)
    sector_ids = jnp.take(slot_sector, slots)
    inverse = jnp.zeros((nsec,), jnp.int32).at[slot_sector].set(jnp.arange(nsec, dtype=jnp.int32))
    source = inverse[couple[sector_ids]]
    rows = block_rows(source, owner, sdev, blk)

    chain = lax.axis_index("chain")
    which = jnp.where(chain == 0, 0, jnp.where(chain % 2 == 1, 1, 2)).astype(jnp.int32).reshape(1)
    terms = lenv.shape[0]

    def in_hbm(value):
        return pltpu.with_memory_space_constraint(value, pltpu.HBM)

    k0, limit, packed = begin(
        owner.astype(jnp.int32).reshape(1),
        *(in_hbm(value) for value in (slot_sector, dims, kept, start)),
    )
    site, k0 = lax.optimization_barrier((site, k0))
    lenv = in_hbm(lenv)
    whole = lax.all_gather(packed, "sector", axis=0, tiled=True)
    some = terms // 8
    sizes = [terms // 2, terms - terms // 2 - 2 * some, some, some]
    built = {}
    for number in (0, 2, 3, 1):
        part = update(lenv, site, sum(sizes[:number]), sizes[number])
        if number < 2:
            near = far = to_next(part)
        else:
            near, far = to_next_round(part)
        built[number] = tuple(in_hbm(value) for value in (part, near, far))
    parts, nears, fars = ([built[number][k] for number in range(len(sizes))] for k in range(3))
    lefts = lenv, nears, fars
    right = in_hbm(renv)

    height = sdev * blk + TAIL
    tails = [device * height + height - TAIL for device in range(devices)]
    first_rows = (source // sdev) * height + (source % sdev) * blk
    known = jnp.zeros((TAIL, blk), jnp.float32)
    known, y0, *quarters = apply(
        first_rows, limit, which, tails, lay([in_hbm(whole)]), [], lefts, right, known, [k0]
    )
    sizes = heights(sdev, blk)
    units = SIDE * SIDE // 2
    tails = [
        half * units * sum(sizes) + unit * sizes[0] + sizes[0] - TAIL
        for half in range(2)
        for unit in range(units)
    ]
    held, came, first = gather(quarters, devices)
    updated = join(parts, first)
    held, came, updated = lax.optimization_barrier((held, came, updated))
    known, z1, *quarters = apply(
        rows, limit, which, tails, held, came, lefts, right, known, [k0, y0]
    )
    held, came, _ = gather(quarters, devices)
    known, x1, r2, sums = apply(
        rows, limit, which, tails, held, came, lefts, right, known, [k0, y0, z1]
    )
    for axis in ("y", "z"):
        others = [swap(sums, (axis, flip), devices) for flip in range(1, SIDE)]
        if axis == "y":
            sums = (sums + others[0]) + (others[1] + others[2])
    x2, energy = finish(jnp.stack([sums] + others), known, x1, r2)
    return (x2[None], updated[None], energy[0, :1])


def solution(mesh):
    placed = (
        P("chain", None, "sector", None, None),
        P("chain", None, "sector", None, None),
        P("chain", "sector", None, None),
        P("chain", "sector", None, None),
        P(),
        P(),
        P(),
        P(),
    )
    return jax.shard_map(
        body,
        mesh=mesh,
        in_specs=placed,
        out_specs=(
            P("chain", "sector", None, None),
            P("chain", None, "sector", None, None),
            P("chain"),
        ),
        check_vma=False,
    )
```
